512 devices in a mesh: seq: 128 (over z, y_lo, x, core), tp: 4 (over y_hi).
Axes of the slice: x: 4, y: 8 (y_hi: 4, y_lo: 2; y = y_hi * 2 + y_lo), z: 8, core: 2. Of those that a mesh axis runs over, the one named last changes fastest.
Arguments:
- token_picks: int32 [2560], replicated, may hold values from 0 to 127, as said below
- live_counts: int32 [128, 2], replicated, may hold values from 1 to 16, as said below
- attn_query: bfloat16 [2560, 1024], P('seq', 'tp'), may hold values from -10 to 10
- attn_key: bfloat16 [2560, 1024], P('seq', 'tp'), may hold values from -10 to 10
- attn_value: bfloat16 [2560, 1024], P('seq', 'tp'), may hold values from -6 to 6
- out_grad: bfloat16 [2560, 2048], P('seq', 'tp'), may hold values from -24 to 24
- out_weight: bfloat16 [1024, 2048], P('tp'), may hold values from -0.1875 to 0.1875
Outputs:
- query_grad: bfloat16 [2560, 1024], P('seq', 'tp')
- key_grad: bfloat16 [2560, 1024], P('seq', 'tp')
- value_grad: bfloat16 [2560, 1024], P('seq', 'tp')
- weight_grad: float32 [1024, 2048], P('tp', 'seq')
The draws below stay inside these ranges and needn't reach their ends.
Inputs may be any that keep to these rules, and one draw needn't show every extreme that they name: `token_picks`: for every index j of seq and each recursion, the first live_counts entries of its list are distinct token positions of shard j in increasing order and the rest are 0; the positions listed for the third recursion are among those listed for the second. `live_counts`: row j holds the used slots of the second and the third recursion of index j; the first lies in 4 to 16 and equals 16 for some j, the second lies in 1 to 4, equals 4 for some j and never exceeds the first.
All inputs are finite; a program needn't handle non-finite values.
Results may differ from the reference program's by a relative error of at most 0.0085.
Values may be sent and summed in bfloat16 or wider, within the bound.
No kernel may reach another device: no remote copies, remote signals or barrier semaphores. Data moves between devices by JAX's collectives and lax.ppermute only.
A program may use at most 64 MiB of HBM per device.

```python
import jax
import jax.numpy as jnp
from jax import lax

D = 2048
HEADS = 8
HS = 128
TOK_DEV = 128
CAP2 = 16
CAP3 = 4
SLOTS = 20
ROWS = 2560
HW = 1024
N_SEQ = 128


def live_lists(key):
    shard_ids = jnp.arange(N_SEQ)
    count_two = jax.random.randint(jax.random.fold_in(key, 201), (N_SEQ,), CAP2 // 4, CAP2 + 1)
    full_two = jax.random.randint(jax.random.fold_in(key, 202), (), 0, N_SEQ)
    count_two = jnp.where(shard_ids == full_two, CAP2, count_two)
    count_three = jax.random.randint(jax.random.fold_in(key, 203), (N_SEQ,), 1, CAP3 + 1)
    full_three = jax.random.randint(jax.random.fold_in(key, 204), (), 0, N_SEQ)
    count_three = jnp.where(shard_ids == full_three, CAP3, count_three)
    shard_keys = jax.random.split(jax.random.fold_in(key, 205), N_SEQ)
    shuffled = jax.vmap(lambda one_key: jax.random.permutation(one_key, TOK_DEV))(shard_keys)
    ranks = jnp.arange(TOK_DEV)[None, :]

    def listed(count_now, capacity):
        marked = jnp.where(ranks < count_now[:, None], shuffled, TOK_DEV + shuffled)
        ordered = jnp.sort(marked, axis=1)[:, :capacity]
        return jnp.where(ordered < TOK_DEV, ordered, 0)
    token_picks = jnp.concatenate([listed(count_two, CAP2), listed(count_three, CAP3)], axis=1)
    live_counts = jnp.stack([count_two, count_three], axis=1)
    return (token_picks.reshape(-1).astype(jnp.int32), live_counts.astype(jnp.int32))


def draw_token_picks(key, part):
    shared = live_lists(key)
    return shared[0]


def draw_live_counts(key, part):
    shared = live_lists(key)
    return shared[1]


def draw_attn_query(key, part):
    key = jax.random.fold_in(key, 11)
    return jax.random.truncated_normal(key, -6.0, 6.0, (ROWS, HW)).astype(jnp.bfloat16)


def draw_attn_key(key, part):
    key = jax.random.fold_in(key, 13)
    return jax.random.truncated_normal(key, -6.0, 6.0, (ROWS, HW)).astype(jnp.bfloat16)


def strengthened(values, own_key, source, target, parts, factor):
    owner, partner = [(jnp.arange(values.shape[axis_at]) // (values.shape[axis_at] // parts)).reshape([-1 if axis == axis_at else 1 for axis in range(values.ndim)]) for axis_at in (source, target)]
    chosen = jax.random.permutation(own_key, parts)[partner]
    strong = (owner == chosen) | (owner == (partner + parts // 2) % parts)
    return jnp.where(strong, factor * values, values)


def levels(own_key, dims, pieces, low, top_value):
    factor_of, own = 1.0, jax.random.fold_in(own_key, 6)
    for axis_at, shards_of in pieces:
        heights = jnp.exp(jax.random.uniform(jax.random.fold_in(own, axis_at), (shards_of,), jnp.float32, low / len(pieces), top_value / len(pieces)))
        factor_of = factor_of * jnp.repeat(heights, dims[axis_at] // shards_of).reshape([-1 if axis == axis_at else 1 for axis in range(len(dims))])
    return factor_of


def gaussian(own_key, shape, scale, bound, cuts=(), kind=jnp.bfloat16):
    factor_of = levels(own_key, shape, cuts, -0.22, 0.18) if cuts else 1.0
    array = jax.random.normal(own_key, shape, jnp.float32) * scale * factor_of
    return jnp.minimum(jnp.maximum(array, -bound), bound).astype(kind)


def bell_draw_with(own_key, extent, width, limit, cuts, heavy, kind=jnp.bfloat16):
    values = width * jax.random.normal(own_key, extent, jnp.float32)
    if cuts:
        values = values * levels(own_key, extent, cuts, -0.22, 0.18)
    return jnp.clip(strengthened(values, jax.random.fold_in(own_key, 3), *heavy), -limit, limit).astype(kind)


def setup_inputs(seed: int = 0) -> dict:
    seeds = jax.random.split(jax.random.key(seed), 8)
    return {
        "token_picks": draw_token_picks(jax.random.fold_in(seeds[7], 71), 0),
        "live_counts": draw_live_counts(jax.random.fold_in(seeds[7], 71), 0),
        "attn_query": draw_attn_query(jax.random.fold_in(seeds[7], 71), 0),
        "attn_key": draw_attn_key(jax.random.fold_in(seeds[7], 71), 0),
        "attn_value": gaussian(seeds[4], (ROWS, HW), 1.0, 6.0, ((0, 128), (1, 4))),
        "out_grad": bell_draw_with(seeds[5], (ROWS, D), 1.0, 24.0, ((0, 128), (1, 4)), (0, 1, 128, 5.5)),
        "out_weight": gaussian(seeds[6], (HW, D), HW ** -0.5, 0.1875, ((0, 4),)),
    }


def tables(token_picks, live_counts, slot_count):
    row_total = token_picks.shape[0]
    row_order = jnp.arange(row_total, dtype=jnp.int32)
    shard_of = row_order // slot_count
    local_slot = row_order % slot_count
    is_third = local_slot >= CAP2
    within = jnp.where(is_third, local_slot - CAP2, local_slot)
    spread = jnp.repeat(live_counts, slot_count, axis=0, total_repeat_length=row_total)
    row_limit = jnp.where(is_third, spread[:, 1], spread[:, 0])
    return shard_of * TOK_DEV + token_picks, is_third, within < row_limit


def permitted(query_side, key_side):
    query_pos, query_third, query_live = query_side
    key_pos, key_third, key_live = key_side
    causal = (key_pos[None, :] <= query_pos[:, None]) | jnp.logical_not(query_live)[:, None]
    return key_live[None, :] & (query_third[:, None] == key_third[None, :]) & causal


def reference(token_picks, live_counts, attn_query, attn_key, attn_value, out_grad, out_weight):
    row_info = tables(token_picks, live_counts, SLOTS)
    allowed = permitted(row_info, row_info)
    score_scale = HS ** -0.5
    grad_rows = jnp.where(row_info[2][:, None], out_grad, jnp.zeros_like(out_grad))
    d_attn = jnp.dot(grad_rows, out_weight.T, preferred_element_type=jnp.float32).astype(jnp.bfloat16)

    def by_head(matrix):
        return matrix.reshape(ROWS, HEADS, HS).transpose(1, 0, 2)

    def one_head(operands):
        queries, keys_head, values_head, grads_head = operands
        scores = jnp.dot(queries, keys_head.T, preferred_element_type=jnp.float32) * score_scale
        scores = jnp.where(allowed, scores, -jnp.inf)
        row_max = jnp.max(scores, axis=1, keepdims=True)
        log_total = row_max + jnp.log(jnp.sum(jnp.exp(scores - row_max), axis=1, keepdims=True))
        prob = jnp.exp(scores - log_total)
        dprob = jnp.dot(grads_head, values_head.T, preferred_element_type=jnp.float32)
        row_delta = jnp.sum(prob * dprob, axis=1, keepdims=True)
        prob_half = prob.astype(jnp.bfloat16)
        attended = jnp.dot(prob_half, values_head, preferred_element_type=jnp.float32).astype(jnp.bfloat16)
        dscore = (prob * (dprob - row_delta)).astype(jnp.bfloat16)
        query_part = (jnp.dot(dscore, keys_head, preferred_element_type=jnp.float32) * score_scale).astype(jnp.bfloat16)
        key_part = (jnp.dot(dscore.T, queries, preferred_element_type=jnp.float32) * score_scale).astype(jnp.bfloat16)
        value_part = jnp.dot(prob_half.T, grads_head, preferred_element_type=jnp.float32).astype(jnp.bfloat16)
        return attended, query_part, key_part, value_part

    results = lax.map(one_head, (by_head(attn_query), by_head(attn_key), by_head(attn_value), by_head(d_attn)))

    def join_heads(stacked):
        return stacked.transpose(1, 0, 2).reshape(ROWS, HW)

    attended = join_heads(results[0])
    weight_grad = jnp.dot(attended.T, grad_rows, preferred_element_type=jnp.float32)
    return (join_heads(results[1]), join_heads(results[2]), join_heads(results[3]), weight_grad)
```

```python
import jax
import jax.numpy as jnp
from jax import lax
from jax.experimental import pallas as pl
from jax.experimental.pallas import tpu as pltpu
from jax.sharding import Mesh
from jax.sharding import PartitionSpec as P

HS = 128
NZ = 8
NA = 16
TP = 4
SLOTS = 20
CAP2 = 16
PAD3 = 8
ROWS = CAP2 + PAD3
WIDTH = 2 * HS
SCALE = HS**-0.5
LOW = -1e30
F32 = jnp.float32
BF16 = jnp.bfloat16

NT = (((1,), (1,)), ((), ()))
NN = (((1,), (0,)), ((), ()))
TN = (((0,), (0,)), ((), ()))


def mm(left, right, dims):
    return lax.dot_general(left, right, dims, preferred_element_type=F32)


def split_rows(block):
    wide = block.astype(F32)
    count, _, width = wide.shape
    second = wide[:, :CAP2].reshape(count * CAP2, width).astype(BF16)
    third = wide[:, CAP2:].reshape(count * PAD3, width).astype(BF16)
    return second, third


def join_rows(second, third, count):
    width = second.shape[1]
    return jnp.concatenate(
        [second.reshape(count, CAP2, width), third.reshape(count, PAD3, width)], axis=1
    )


def allowed(counts_ref, which, slots, z_own, a_own):
    shape = (NZ * slots, NA * slots)
    key_row = lax.broadcasted_iota(jnp.int32, shape, 0)
    query_row = lax.broadcasted_iota(jnp.int32, shape, 1)
    key_z = key_row // slots
    key_slot = key_row % slots
    key_order = (key_z * NA + a_own) * slots + key_slot
    query_order = z_own * NA * slots + query_row
    limit = jnp.concatenate(
        [
            jnp.full((slots, NA * slots), counts_ref[z * NA + a_own, which], jnp.int32)
            for z in range(NZ)
        ],
        axis=0,
    )
    return (key_order <= query_order) & (key_slot < limit)


def project_kernel(place_ref, counts_ref, grad_ref, weight_ref, query_ref, key_ref, value_ref, qd_ref, kvg_ref):
    shard = place_ref[0] * NA + place_ref[1]
    slot = lax.broadcasted_iota(jnp.int32, (SLOTS, 512), 0)
    live = slot < jnp.where(slot < CAP2, counts_ref[shard, 0], CAP2 + counts_ref[shard, 1])
    total = jnp.zeros((SLOTS, WIDTH), F32)
    pieces = []
    for t in range(TP):
        piece = jnp.where(live, grad_ref[t].astype(F32), 0.0).astype(BF16)
        pieces.append(piece)
        total += mm(piece, weight_ref[:, t * 512 : (t + 1) * 512], NT)
    rest = jnp.zeros((ROWS - SLOTS, WIDTH), F32)

    def padded(block):
        return jnp.concatenate([block.astype(F32), rest], axis=0).astype(BF16)

    query = padded(query_ref[...])
    d_attn = padded(total.astype(BF16))
    key = padded(key_ref[...])
    value = padded(value_ref[...])
    for a in range(NA):
        qd_ref[a, :, :WIDTH] = query
        qd_ref[a, :, WIDTH:] = d_attn
    for z in range(NZ):
        kvg_ref[z, :, :WIDTH] = key
        kvg_ref[z, :, WIDTH : 2 * WIDTH] = value
        column = z * WIDTH
        kvg_ref[z, :, 2 * WIDTH :] = padded(pieces[column // 512][:, column % 512 : column % 512 + WIDTH])


def groups(kv, qd):
    kv_parts = split_rows(kv)
    qd_parts = split_rows(qd)
    return [(0, CAP2, kv_parts[0], qd_parts[0]), (1, PAD3, kv_parts[1], qd_parts[1])]


def stats_kernel(place_ref, counts_ref, kvg_ref, qd_ref, out_ref):
    z_own, a_own = place_ref[0], place_ref[1]
    rows = {}
    attended = {}
    for which, slots, kv, qd in groups(kvg_ref[:, :, : 2 * WIDTH], qd_ref[...]):
        mask = allowed(counts_ref, which, slots, z_own, a_own)
        for h in range(2):
            cols = slice(h * HS, (h + 1) * HS)
            cols2 = slice(WIDTH + h * HS, WIDTH + (h + 1) * HS)
            scores = jnp.where(mask, mm(kv[:, cols], qd[:, cols], NT) * SCALE, LOW)
            top = jnp.max(scores, axis=0, keepdims=True)
            weights = jnp.where(mask, jnp.exp(scores - top), 0.0)
            total = jnp.sum(weights, axis=0, keepdims=True)
            none = total == 0.0
            inverse = 1.0 / jnp.where(none, 1.0, total)
            weights = weights * inverse
            dprob = mm(kv[:, cols2], qd[:, cols2], NT)
            rows[which, h, 0] = jnp.where(none, LOW, top + jnp.log(jnp.where(none, 1.0, total)))
            rows[which, h, 1] = jnp.sum(weights * dprob, axis=0, keepdims=True)
            attended[which, h] = mm(weights.astype(BF16), kv[:, cols2], TN)
    for h in range(2):
        out_ref[:, :ROWS, h * HS : (h + 1) * HS] = join_rows(attended[0, h], attended[1, h], NA)
    stats = jnp.concatenate(
        [
            rows[0, 0, 0],
            rows[0, 1, 0],
            rows[0, 0, 1],
            rows[0, 1, 1],
            jnp.concatenate([rows[1, 0, 0], rows[1, 1, 0]], axis=1),
            jnp.concatenate([rows[1, 0, 1], rows[1, 1, 1]], axis=1),
            jnp.zeros((2, WIDTH), F32),
        ],
        axis=0,
    )
    for a in range(NA):
        out_ref[a, ROWS:, :] = stats


def grads_kernel(place_ref, counts_ref, kvg_ref, qd_ref, in_ref, out_ref, dq_ref, share2_ref, share3_ref):
    z_own, a_own = place_ref[0], place_ref[1]
    stat = {}
    for h in range(2):
        stat[0, h] = (in_ref[:, ROWS + h, :], in_ref[:, ROWS + 2 + h, :])
        cols = slice(h * HS, (h + 1) * HS)
        stat[1, h] = (in_ref[:, ROWS + 4, cols], in_ref[:, ROWS + 5, cols])
    log_total, delta = {}, {}
    for (which, h), (logs, deltas) in stat.items():
        top = jnp.max(logs, axis=0, keepdims=True)
        whole = top + jnp.log(jnp.sum(jnp.exp(logs - top), axis=0, keepdims=True))
        share = jnp.exp(logs - whole)
        log_total[which, h] = whole
        delta[which, h] = jnp.sum(share * deltas, axis=0, keepdims=True)
        if which == 0:
            share2_ref[h] = share.T
        else:
            share3_ref[h] = share.T
    own2 = pl.ds(pl.multiple_of(a_own * CAP2, CAP2), CAP2)
    own3 = pl.ds(pl.multiple_of(a_own * PAD3, PAD3), PAD3)
    attended = []
    for h in range(2):
        share = jnp.concatenate([share2_ref[h, own2, :], share3_ref[h, own3, :]], axis=0)
        cols = slice(h * HS, (h + 1) * HS)
        total = jnp.zeros((ROWS, HS), F32)
        for a in range(NA):
            total += share[:, a : a + 1] * in_ref[a, :ROWS, cols]
        attended.append(total.astype(BF16))
    attended = jnp.concatenate(attended, axis=1)

    d_query, d_key, d_value = {}, {}, {}
    for which, slots, kv, qd in groups(kvg_ref[:, :, : 2 * WIDTH], qd_ref[...]):
        mask = allowed(counts_ref, which, slots, z_own, a_own)
        for h in range(2):
            cols = slice(h * HS, (h + 1) * HS)
            cols2 = slice(WIDTH + h * HS, WIDTH + (h + 1) * HS)
            scores = mm(kv[:, cols], qd[:, cols], NT) * SCALE
            prob = jnp.where(mask, jnp.exp(jnp.where(mask, scores, LOW) - log_total[which, h]), 0.0)
            dprob = mm(kv[:, cols2], qd[:, cols2], NT)
            dscore = (prob * (dprob - delta[which, h])).astype(BF16)
            d_value[which, h] = mm(prob.astype(BF16), qd[:, cols2], NN)
            d_key[which, h] = mm(dscore, qd[:, cols], NN) * SCALE
            d_query[which, h] = mm(dscore, kv[:, cols], TN) * SCALE
    for h in range(2):
        cols = slice(h * HS, (h + 1) * HS)
        cols2 = slice(WIDTH + h * HS, WIDTH + (h + 1) * HS)
        out_ref[:, :, cols] = join_rows(d_key[0, h], d_key[1, h], NZ).astype(BF16)
        out_ref[:, :, cols2] = join_rows(d_value[0, h], d_value[1, h], NZ).astype(BF16)
        dq_ref[:, :, cols] = join_rows(d_query[0, h], d_query[1, h], NA)
    for z in range(NZ):
        out_ref[z, :, 2 * WIDTH :] = attended


def weight_kernel(in_ref, kvg_ref, dq_ref, dk_ref, dv_ref, out_ref):
    total = jnp.sum(in_ref[:, :, : 2 * WIDTH].astype(F32), axis=0)
    dk_ref[...] = total[:SLOTS, :WIDTH].astype(BF16)
    dv_ref[...] = total[:SLOTS, WIDTH:].astype(BF16)
    attended = in_ref[:, :, 2 * WIDTH :].astype(F32).reshape(NZ * ROWS, WIDTH).astype(BF16)
    columns = kvg_ref[:, :, 2 * WIDTH :].astype(F32).reshape(NZ * ROWS, WIDTH).astype(BF16)
    part = mm(columns, attended, TN)
    out_ref[:, :ROWS, :] = dq_ref[...]
    out_ref[:, ROWS:, :] = part.reshape(NA, WIDTH // NA, WIDTH)


def last_kernel(in_ref, dq_ref, dw_ref):
    total = jnp.sum(in_ref[...], axis=0)
    dq_ref[...] = total[:SLOTS].astype(BF16)
    dw_ref[...] = total[ROWS:]


def on_device(token_picks, live_counts, attn_query, attn_key, attn_value, out_grad, out_weight):
    del token_picks
    place = jnp.stack([lax.axis_index("z"), lax.axis_index("a")]).astype(jnp.int32)
    smem = pl.BlockSpec(memory_space=pltpu.SMEM)
    vmem = pl.BlockSpec(memory_space=pltpu.VMEM)

    def run(kernel, outs, args, scratch=(), scalars=2):
        return pl.pallas_call(
            kernel,
            out_shape=[jax.ShapeDtypeStruct(*o) for o in outs],
            in_specs=[smem] * scalars + [vmem] * (len(args) - scalars),
            out_specs=[vmem] * len(outs),
            scratch_shapes=list(scratch),
            compiler_params=pltpu.CompilerParams(vmem_limit_bytes=32 * 2**20),
        )(*args)

    grad = lax.all_gather(out_grad, "tp", axis=0, tiled=False)
    qd, kvg = run(
        project_kernel,
        [((NA, ROWS, 2 * WIDTH), BF16), ((NZ, ROWS, 3 * WIDTH), BF16)],
        (place, live_counts, grad, out_weight, attn_query, attn_key, attn_value),
    )
    kvg = lax.all_to_all(kvg, "z", 0, 0)
    qd = lax.all_to_all(qd, "a", 0, 0)
    (stats,) = run(stats_kernel, [((NA, ROWS + 8, WIDTH), F32)], (place, live_counts, kvg, qd))
    stats = lax.all_to_all(stats, "a", 0, 0)
    back, dq = run(
        grads_kernel,
        [((NZ, ROWS, 3 * WIDTH), BF16), ((NA, ROWS, WIDTH), F32)],
        (place, live_counts, kvg, qd, stats),
        [pltpu.VMEM((2, NA * CAP2, NA), F32), pltpu.VMEM((2, NA * PAD3, NA), F32)],
    )
    back = lax.all_to_all(back, "z", 0, 0)
    key_grad, value_grad, last = run(
        weight_kernel,
        [((SLOTS, WIDTH), BF16), ((SLOTS, WIDTH), BF16), ((NA, ROWS + WIDTH // NA, WIDTH), F32)],
        (back, kvg, dq),
        scalars=0,
    )
    last = lax.all_to_all(last, "a", 0, 0)
    query_grad, weight_grad = run(
        last_kernel, [((SLOTS, WIDTH), BF16), ((WIDTH // NA, WIDTH), F32)], (last,), scalars=0
    )
    return query_grad, key_grad, value_grad, weight_grad.T


def solution(mesh):
    grid = Mesh(mesh.devices.reshape(NZ, NA, TP), ("z", "a", "tp"))
    rows = P(("z", "a"), "tp")
    return jax.shard_map(
        on_device,
        mesh=grid,
        in_specs=(P(), P(), rows, rows, rows, rows, P("tp", None)),
        out_specs=(rows, rows, rows, P("tp", ("z", "a"))),
        check_vma=False,
    )
```

```python
import jax
import jax.numpy as jnp
from jax import lax
from jax.experimental import pallas as pl
from jax.experimental.pallas import tpu as pltpu
from jax.sharding import Mesh
from jax.sharding import PartitionSpec as P

HS = 128
NZ, NY, NX, NC = 8, 2, 4, 2
FAR = ("z", "x")
NEAR = ("y", "c")
NF, NN_ = NZ * NX, NY * NC
TP = 4
SLOTS = 20
CAP2 = 16
CAP3 = 4
PAD3 = 8
ROWS = CAP2 + PAD3
WIDTH = 2 * HS
MODEL = 2048
COLS = MODEL // 128
QROWS = NN_ * ROWS
BACK = 2 * CAP2 + PAD3 + COLS
SCALE = HS**-0.5
LOW = -1e30
F32 = jnp.float32
BF16 = jnp.bfloat16

NT = (((1,), (1,)), ((), ()))
NN = (((1,), (0,)), ((), ()))
TN = (((0,), (0,)), ((), ()))


def mm(left, right, dims):
    return lax.dot_general(left, right, dims, preferred_element_type=F32)


def split_rows(block):
    wide = block.astype(F32)
    count, _, width = wide.shape
    second = wide[:, :CAP2].reshape(count * CAP2, width).astype(BF16)
    third = wide[:, CAP2:].reshape(count * PAD3, width).astype(BF16)
    return second, third


def by_head(rows):
    column = lax.broadcasted_iota(jnp.int32, rows.shape, 1)
    zero = jnp.zeros_like(rows)
    return jnp.concatenate(
        [jnp.where(column < HS, rows, zero), jnp.where(column < HS, zero, rows)], axis=0
    )


def head_blocks(both):
    count = both.shape[0] // 2
    column = lax.broadcasted_iota(jnp.int32, (count, WIDTH), 1)
    return jnp.where(column < HS, both[:count], both[count:])


def allowed(place_ref, counts_ref, which, slots):
    z, y, x, c = (place_ref[i] for i in range(4))
    shape = (NF * slots, 2 * NN_ * slots)
    key_row = lax.broadcasted_iota(jnp.int32, shape, 0)
    query_row = lax.broadcasted_iota(jnp.int32, shape, 1) % (NN_ * slots)
    key_far, key_slot = key_row // slots, key_row % slots
    key_shard = (((key_far // NX) * NY + y) * NX + key_far % NX) * NC + c
    near, query_slot = query_row // slots, query_row % slots
    query_shard = ((z * NY + near // NC) * NX + x) * NC + near % NC
    limit = jnp.concatenate(
        [
            jnp.full((slots, shape[1]), counts_ref[which, ((f // NX * NY + y) * NX + f % NX) * NC + c], jnp.int32)
            for f in range(NF)
        ],
        axis=0,
    )
    in_order = key_shard * slots + key_slot <= query_shard * slots + query_slot
    return in_order & (key_slot < limit)


def blocks(kv_ref, qd_ref):
    kv_parts = split_rows(kv_ref[...])
    qd_parts = split_rows(qd_ref[:, :, : 2 * WIDTH])
    found = []
    for which, slots in ((0, CAP2), (1, PAD3)):
        kv, qd = kv_parts[which], qd_parts[which]
        found.append(
            (which, slots, kv[:, :WIDTH], kv[:, WIDTH:], by_head(qd[:, :WIDTH]), by_head(qd[:, WIDTH:]))
        )
    return found


def padded(block):
    rest = jnp.zeros((ROWS - SLOTS, block.shape[1]), F32)
    return jnp.concatenate([block.astype(F32), rest], axis=0).astype(BF16)


def project_kernel(place_ref, counts_ref, grad_ref, weight_ref, query_ref, out_ref):
    z, y, x, c = (place_ref[i] for i in range(4))
    shard = ((z * NY + y) * NX + x) * NC + c
    slot = lax.broadcasted_iota(jnp.int32, (SLOTS, 512), 0)
    live = slot < jnp.where(slot < CAP2, counts_ref[0, shard], CAP2 + counts_ref[1, shard])
    total = jnp.zeros((SLOTS, WIDTH), F32)
    for t in range(TP):
        piece = jnp.where(live, grad_ref[t].astype(F32), 0.0).astype(BF16)
        total += mm(piece, weight_ref[:, t * 512 : (t + 1) * 512], NT)
        out_ref[:, 2 * WIDTH + t * 512 : 2 * WIDTH + (t + 1) * 512] = padded(piece)
    out_ref[:, :WIDTH] = padded(query_ref[...])
    out_ref[:, WIDTH : 2 * WIDTH] = padded(total.astype(BF16))


def stats_kernel(place_ref, counts_ref, kv_ref, qd_ref, out_ref):
    start = 0
    stats = []
    for which, slots, key, value, query, d_attn in blocks(kv_ref, qd_ref):
        mask = allowed(place_ref, counts_ref, which, slots)
        scores = jnp.where(mask, mm(key, query, NT) * SCALE, LOW)
        top = jnp.max(scores, axis=0, keepdims=True)
        weights = jnp.where(mask, jnp.exp(scores - top), 0.0)
        total = jnp.sum(weights, axis=0, keepdims=True)
        none = total == 0.0
        weights = weights * (1.0 / jnp.where(none, 1.0, total))
        logs = jnp.where(none, LOW, top + jnp.log(jnp.where(none, 1.0, total)))
        delta = jnp.sum(weights * mm(value, d_attn, NT), axis=0, keepdims=True)
        attended = head_blocks(mm(weights.astype(BF16), value, TN))
        out_ref[start : start + NN_ * slots] = attended
        start += NN_ * slots
        rest = jnp.zeros((1, WIDTH - logs.shape[1]), F32)
        stats += [jnp.concatenate([logs, rest], axis=1), jnp.concatenate([delta, rest], axis=1)]
    out_ref[start:] = jnp.concatenate(stats + [jnp.zeros((8 - len(stats), WIDTH), F32)], axis=0)


def grads_kernel(place_ref, counts_ref, kv_ref, qd_ref, in_ref, out_ref, dq_ref):
    y, c = place_ref[1], place_ref[3]
    attended = []
    d_key, d_value = [], []
    start = 0
    for which, slots, key, value, query, d_attn in blocks(kv_ref, qd_ref):
        count = NN_ * slots
        logs = in_ref[:, QROWS + 2 * which, : 2 * count]
        deltas = in_ref[:, QROWS + 2 * which + 1, : 2 * count]
        top = jnp.max(logs, axis=0, keepdims=True)
        log_total = top + jnp.log(jnp.sum(jnp.exp(logs - top), axis=0, keepdims=True))
        share = jnp.exp(logs - log_total)
        delta = jnp.sum(share * deltas, axis=0, keepdims=True)
        share_down = jnp.concatenate([share, jnp.zeros((8 - NN_, 2 * count), F32)], axis=0).T
        column = lax.broadcasted_iota(jnp.int32, (count, WIDTH), 1)
        total = jnp.zeros((count, WIDTH), F32)
        for n in range(NN_):
            own = jnp.where(column < HS, share_down[:count, n : n + 1], share_down[count:, n : n + 1])
            total += own * in_ref[n, start : start + count]
        attended.append(total)

        mask = allowed(place_ref, counts_ref, which, slots)
        scores = jnp.where(mask, mm(key, query, NT) * SCALE, LOW)
        prob = jnp.where(mask, jnp.exp(scores - log_total), 0.0)
        dscore = (prob * (mm(value, d_attn, NT) - delta)).astype(BF16)
        d_value.append(mm(prob.astype(BF16), d_attn, NN).reshape(NF, slots, WIDTH))
        d_key.append((mm(dscore, query, NN) * SCALE).reshape(NF, slots, WIDTH))
        dq_ref[start : start + count] = head_blocks(mm(dscore, key, TN)) * SCALE
        start += count
    out_ref[:, :CAP2] = d_key[0].astype(BF16)
    out_ref[:, CAP2 : 2 * CAP2] = d_value[0].astype(BF16)
    attended = jnp.concatenate(attended, axis=0).astype(BF16)
    parts = []
    for z in range(NZ):
        column = pl.multiple_of(2 * WIDTH + (z * NY + y) * HS, HS)
        second, third = split_rows(qd_ref[:, :, pl.ds(column, HS)])
        grad = jnp.concatenate([second, third], axis=0)
        parts.append(mm(grad, attended, TN).reshape(NX, NC, COLS, WIDTH))
    parts = jnp.concatenate(parts, axis=0)
    own = jnp.where(c == 0, parts[:, 0], parts[:, 1])
    third = jnp.concatenate([d_key[1][:, :CAP3], d_value[1][:, :CAP3]], axis=1)
    out_ref[:, 2 * CAP2 :] = jnp.concatenate([third, own], axis=1).astype(BF16)


def query_kernel(place_ref, in_ref, dq_ref):
    near = place_ref[1] * NC + place_ref[3]
    second = pl.ds(pl.multiple_of(near * CAP2, CAP2), CAP2)
    third = pl.ds(pl.multiple_of(NN_ * CAP2 + near * PAD3, PAD3), PAD3)
    total = jnp.concatenate(
        [jnp.sum(in_ref[:, second, :], axis=0), jnp.sum(in_ref[:, third, :], axis=0)[:CAP3]], axis=0
    )
    dq_ref[...] = total.astype(BF16)


def last_kernel(in_ref, dk_ref, dv_ref, dw_ref):
    total = jnp.sum(in_ref[...].astype(F32), axis=0)
    third = 2 * CAP2
    dk_ref[...] = jnp.concatenate([total[:CAP2], total[third : third + CAP3]], axis=0).astype(BF16)
    dv_ref[...] = jnp.concatenate(
        [total[CAP2 : 2 * CAP2], total[third + CAP3 : third + 2 * CAP3]], axis=0
    ).astype(BF16)
    dw_ref[...] = total[third + PAD3 :]


def on_device(token_picks, live_counts, attn_query, attn_key, attn_value, out_grad, out_weight):
    del token_picks
    place = jnp.stack([lax.axis_index(a) for a in ("z", "y", "x", "c")]).astype(jnp.int32)
    smem = pl.BlockSpec(memory_space=pltpu.SMEM)
    vmem = pl.BlockSpec(memory_space=pltpu.VMEM)

    def run(kernel, outs, args, scalars):
        return pl.pallas_call(
            kernel,
            out_shape=[jax.ShapeDtypeStruct(*o) for o in outs],
            in_specs=[smem] * scalars + [vmem] * (len(args) - scalars),
            out_specs=[vmem] * len(outs),
            compiler_params=pltpu.CompilerParams(vmem_limit_bytes=32 * 2**20),
        )(*args)

    live_counts = live_counts.T
    kv = jnp.pad(jnp.concatenate([attn_key, attn_value], axis=1), ((0, ROWS - SLOTS), (0, 0)))
    kv = jnp.broadcast_to(kv[None], (NF, ROWS, 2 * WIDTH))
    kv = lax.all_to_all(kv, FAR, 0, 0)
    grad = lax.all_gather(out_grad, "tp", axis=0, tiled=False)
    (qd,) = run(
        project_kernel,
        [((ROWS, 2 * WIDTH + MODEL), BF16)],
        (place, live_counts, grad, out_weight, attn_query),
        2,
    )
    qd = lax.all_gather(qd, NEAR, axis=0, tiled=False)
    (stats,) = run(stats_kernel, [((QROWS + 8, WIDTH), F32)], (place, live_counts, kv, qd), 2)
    stats = lax.all_gather(stats, NEAR, axis=0, tiled=False)
    back, dq = run(
        grads_kernel,
        [((NF, BACK, WIDTH), BF16), ((QROWS, WIDTH), F32)],
        (place, live_counts, kv, qd, stats),
        2,
    )
    back = lax.all_to_all(back, FAR, 0, 0)
    dq = lax.all_gather(dq, NEAR, axis=0, tiled=False)
    (query_grad,) = run(query_kernel, [((SLOTS, WIDTH), BF16)], (place, dq), 1)
    key_grad, value_grad, weight_grad = run(
        last_kernel,
        [((SLOTS, WIDTH), BF16), ((SLOTS, WIDTH), BF16), ((COLS, WIDTH), F32)],
        (back,),
        0,
    )
    return query_grad, key_grad, value_grad, weight_grad.T


def solution(mesh):
    grid = Mesh(mesh.devices.reshape(NZ, NY, NX, NC, TP), ("z", "y", "x", "c", "tp"))
    seq = ("z", "y", "x", "c")
    rows = P(seq, "tp")
    return jax.shard_map(
        on_device,
        mesh=grid,
        in_specs=(P(), P(), rows, rows, rows, rows, P("tp", None)),
        out_specs=(rows, rows, rows, P("tp", seq)),
        check_vma=False,
    )
```

```python
import jax
import jax.numpy as jnp
from jax import lax
from jax.experimental import pallas as pl
from jax.experimental.pallas import tpu as pltpu
from jax.sharding import Mesh
from jax.sharding import PartitionSpec as P

HS = 128
NZ, NY, NX, NC = 8, 2, 4, 2
FAR = ("z", "x")
NEAR = ("y", "c")
NF, NEARS = NZ * NX, NY * NC
TP = 4
SLOTS = 20
CAP2 = 16
CAP3 = 4
PAD3 = 8
ROWS = CAP2 + PAD3
WIDTH = 2 * HS
MODEL = 2048
COLS = MODEL // 128
QROWS = NEARS * ROWS
BACK = 2 * CAP2 + PAD3 + COLS
SCALE = HS**-0.5
LOW = -1e30
F32 = jnp.float32
BF16 = jnp.bfloat16

NT = (((1,), (1,)), ((), ()))
NN = (((1,), (0,)), ((), ()))
TN = (((0,), (0,)), ((), ()))


def mm(left, right, dims):
    return lax.dot_general(left, right, dims, preferred_element_type=F32)


def split_rows(block):
    wide = block.astype(F32)
    count, _, width = wide.shape
    second = wide[:, :CAP2].reshape(count * CAP2, width).astype(BF16)
    third = wide[:, CAP2:].reshape(count * PAD3, width).astype(BF16)
    return second, third


def by_head(rows):
    column = lax.broadcasted_iota(jnp.int32, rows.shape, 1)
    zero = jnp.zeros_like(rows)
    return jnp.concatenate(
        [jnp.where(column < HS, rows, zero), jnp.where(column < HS, zero, rows)], axis=0
    )


def head_blocks(both):
    count = both.shape[0] // 2
    column = lax.broadcasted_iota(jnp.int32, (count, WIDTH), 1)
    return jnp.where(column < HS, both[:count], both[count:])


def shard_of(z, y, x, c):
    return ((z * NY + y) * NX + x) * NC + c


def place():
    return tuple(lax.axis_index(axis) for axis in ("z", "y", "x", "c"))


def allowed(limit_ref, which, slots):
    z, y, x, c = place()
    shape = (NF * slots, 2 * NEARS * slots)
    key_row = lax.broadcasted_iota(jnp.int32, shape, 0)
    query_row = lax.broadcasted_iota(jnp.int32, shape, 1) % (NEARS * slots)
    key_far, key_slot = key_row // slots, key_row % slots
    key_shard = shard_of(key_far // NX, y, key_far % NX, c)
    near, query_slot = query_row // slots, query_row % slots
    query_shard = shard_of(z, near // NC, x, near % NC)
    limit = limit_ref[which * NF : (which + 1) * NF, : shape[1]]
    limit = jnp.broadcast_to(limit[:, None, :], (NF, slots, shape[1])).reshape(shape)
    in_order = key_shard * slots + key_slot <= query_shard * slots + query_slot
    return in_order & (key_slot < limit)


def blocks(kv_ref, qd_ref):
    kv = kv_ref[...].astype(F32)
    third = kv[:, 2 * CAP2 :]
    shifted = jnp.concatenate([third[:, CAP3:], third[:, :CAP3]], axis=1)
    pairs = ((kv[:, :CAP2], kv[:, CAP2 : 2 * CAP2]), (third, shifted))
    qd_parts = split_rows(qd_ref[:, :, : 2 * WIDTH])
    found = []
    for which, slots in ((0, CAP2), (1, PAD3)):
        key, value = (part.reshape(NF * slots, WIDTH).astype(BF16) for part in pairs[which])
        qd = qd_parts[which]
        found.append((which, slots, key, value, by_head(qd[:, :WIDTH]), by_head(qd[:, WIDTH:])))
    return found


def padded(block):
    rest = jnp.zeros((ROWS - SLOTS, block.shape[1]), F32)
    return jnp.concatenate([block.astype(F32), rest], axis=0).astype(BF16)


def start_kernel(
    counts_any, key_any, value_any, grad_any, kv_any, grad_ref, limit_ref, counts, key, value, grad, block, sems, out_sems
):
    moves = [
        pltpu.make_async_copy(source, target, sems.at[i])
        for i, (source, target) in enumerate(
            ((key_any, key), (value_any, value), (counts_any, counts), (grad_any, grad))
        )
    ]
    for move in moves:
        move.start()
    moves[0].wait()
    moves[1].wait()
    keys, values = key[...].astype(F32), value[...].astype(F32)
    block[...] = jnp.concatenate(
        [keys[:CAP2], values[:CAP2], keys[CAP2:], values[CAP2:]], axis=0
    ).astype(BF16)
    sends = [pltpu.make_async_copy(block, kv_any.at[f], out_sems.at[f]) for f in range(NF)]
    for send in sends:
        send.start()
    moves[2].wait()
    moves[3].wait()
    z, y, x, c = place()
    shard = shard_of(z, y, x, c)
    slot = lax.broadcasted_iota(jnp.int32, (SLOTS, 512), 0)
    live = slot < jnp.where(slot < CAP2, counts[0, shard], CAP2 + counts[1, shard])
    grad_ref[...] = jnp.where(live, grad[...].astype(F32), 0.0).astype(BF16)
    for which in range(2):
        for f in range(NF):
            limit = counts[which, shard_of(f // NX, y, f % NX, c)]
            limit_ref[which * NF + f : which * NF + f + 1, :] = jnp.full((1, HS), limit, jnp.int32)
    for send in sends:
        send.wait()


def project_kernel(grad_ref, weight_ref, query_ref, out_ref):
    total = jnp.zeros((SLOTS, WIDTH), F32)
    for t in range(TP):
        piece = grad_ref[t]
        total += mm(piece, weight_ref[:, t * 512 : (t + 1) * 512], NT)
        out_ref[:, 2 * WIDTH + t * 512 : 2 * WIDTH + (t + 1) * 512] = padded(piece)
    out_ref[:, :WIDTH] = padded(query_ref[...])
    out_ref[:, WIDTH : 2 * WIDTH] = padded(total.astype(BF16))


def stats_kernel(limit_ref, kv_ref, qd_ref, out_ref, *kept):
    start = 0
    stats = []
    for which, slots, key, value, query, d_attn in blocks(kv_ref, qd_ref):
        mask = allowed(limit_ref, which, slots)
        scores = jnp.where(mask, mm(key, query, NT) * SCALE, LOW)
        dprob = mm(value, d_attn, NT)
        kept[2 * which][...] = scores
        kept[2 * which + 1][...] = dprob
        top = jnp.max(scores, axis=0, keepdims=True)
        weights = jnp.where(mask, jnp.exp(scores - top), 0.0)
        total = jnp.sum(weights, axis=0, keepdims=True)
        none = total == 0.0
        weights = weights * (1.0 / jnp.where(none, 1.0, total))
        logs = jnp.where(none, LOW, top + jnp.log(jnp.where(none, 1.0, total)))
        delta = jnp.sum(weights * dprob, axis=0, keepdims=True)
        attended = head_blocks(mm(weights.astype(BF16), value, TN))
        out_ref[start : start + NEARS * slots] = attended
        start += NEARS * slots
        rest = jnp.zeros((1, WIDTH - logs.shape[1]), F32)
        stats += [jnp.concatenate([logs, rest], axis=1), jnp.concatenate([delta, rest], axis=1)]
    out_ref[start:] = jnp.concatenate(stats + [jnp.zeros((8 - len(stats), WIDTH), F32)], axis=0)


def grads_kernel(kv_ref, qd_ref, in_ref, *refs):
    kept, (out_ref, dq_ref) = refs[:4], refs[4:]
    _, y, _, c = place()
    attended = []
    d_key, d_value = [], []
    start = 0
    for which, slots, key, _, query, d_attn in blocks(kv_ref, qd_ref):
        count = NEARS * slots
        logs = in_ref[:, QROWS + 2 * which, : 2 * count]
        deltas = in_ref[:, QROWS + 2 * which + 1, : 2 * count]
        top = jnp.max(logs, axis=0, keepdims=True)
        log_total = top + jnp.log(jnp.sum(jnp.exp(logs - top), axis=0, keepdims=True))
        share = jnp.exp(logs - log_total)
        delta = jnp.sum(share * deltas, axis=0, keepdims=True)
        share_down = jnp.concatenate([share, jnp.zeros((8 - NEARS, 2 * count), F32)], axis=0).T
        column = lax.broadcasted_iota(jnp.int32, (count, WIDTH), 1)
        total = jnp.zeros((count, WIDTH), F32)
        for n in range(NEARS):
            own = jnp.where(column < HS, share_down[:count, n : n + 1], share_down[count:, n : n + 1])
            total += own * in_ref[n, start : start + count]
        attended.append(total)

        prob = jnp.exp(kept[2 * which][...] - log_total)
        dscore = (prob * (kept[2 * which + 1][...] - delta)).astype(BF16)
        d_value.append(mm(prob.astype(BF16), d_attn, NN).reshape(NF, slots, WIDTH))
        d_key.append((mm(dscore, query, NN) * SCALE).reshape(NF, slots, WIDTH))
        dq_ref[start : start + count] = head_blocks(mm(dscore, key, TN)) * SCALE
        start += count
    out_ref[:, :CAP2] = d_key[0].astype(BF16)
    out_ref[:, CAP2 : 2 * CAP2] = d_value[0].astype(BF16)
    attended = jnp.concatenate(attended, axis=0).astype(BF16)
    parts = []
    for z in range(NZ):
        column = pl.multiple_of(2 * WIDTH + (z * NY + y) * HS, HS)
        second, third = split_rows(qd_ref[:, :, pl.ds(column, HS)])
        grad = jnp.concatenate([second, third], axis=0)
        parts.append(mm(grad, attended, TN).reshape(NX, NC, COLS, WIDTH))
    parts = jnp.concatenate(parts, axis=0)
    own = jnp.where(c == 0, parts[:, 0], parts[:, 1])
    third = jnp.concatenate([d_key[1][:, :CAP3], d_value[1][:, :CAP3]], axis=1)
    out_ref[:, 2 * CAP2 :] = jnp.concatenate([third, own], axis=1).astype(BF16)


def query_kernel(in_ref, dq_ref):
    _, y, _, c = place()
    near = y * NC + c
    second = pl.ds(pl.multiple_of(near * CAP2, CAP2), CAP2)
    third = pl.ds(pl.multiple_of(NEARS * CAP2 + near * PAD3, PAD3), PAD3)
    total = jnp.concatenate(
        [jnp.sum(in_ref[:, second, :], axis=0), jnp.sum(in_ref[:, third, :], axis=0)[:CAP3]], axis=0
    )
    dq_ref[...] = total.astype(BF16)


def last_kernel(in_ref, dk_ref, dv_ref, dw_ref):
    total = jnp.sum(in_ref[...].astype(F32), axis=0)
    third = 2 * CAP2
    dk_ref[...] = jnp.concatenate([total[:CAP2], total[third : third + CAP3]], axis=0).astype(BF16)
    dv_ref[...] = jnp.concatenate(
        [total[CAP2 : 2 * CAP2], total[third + CAP3 : third + 2 * CAP3]], axis=0
    ).astype(BF16)
    dw_ref[...] = total[third + PAD3 :]


def on_device(token_picks, live_counts, attn_query, attn_key, attn_value, out_grad, out_weight):
    del token_picks
    vmem = pl.BlockSpec(memory_space=pltpu.VMEM)
    anywhere = pl.BlockSpec(memory_space=pl.ANY)
    parameters = pltpu.CompilerParams(vmem_limit_bytes=32 * 2**20)

    def run(kernel, outs, args):
        return pl.pallas_call(
            kernel,
            out_shape=[jax.ShapeDtypeStruct(*o) for o in outs],
            in_specs=[vmem] * len(args),
            out_specs=[vmem] * len(outs),
            compiler_params=parameters,
        )(*args)

    live_counts = live_counts.T
    kv, out_grad, limits = pl.pallas_call(
        start_kernel,
        out_shape=[
            jax.ShapeDtypeStruct((NF, 2 * SLOTS, WIDTH), BF16),
            jax.ShapeDtypeStruct(out_grad.shape, BF16),
            jax.ShapeDtypeStruct((2 * NF, HS), jnp.int32),
        ],
        in_specs=[anywhere] * 4,
        out_specs=[anywhere, vmem, vmem],
        scratch_shapes=[
            pltpu.SMEM(live_counts.shape, jnp.int32),
            pltpu.VMEM((SLOTS, WIDTH), BF16),
            pltpu.VMEM((SLOTS, WIDTH), BF16),
            pltpu.VMEM(out_grad.shape, BF16),
            pltpu.VMEM((2 * SLOTS, WIDTH), BF16),
            pltpu.SemaphoreType.DMA((4,)),
            pltpu.SemaphoreType.DMA((NF,)),
        ],
    )(live_counts, attn_key, attn_value, out_grad)
    kv = lax.all_to_all(kv, FAR, 0, 0)
    grad = lax.all_gather(out_grad[None], "tp", axis=0, tiled=True, axis_index_groups=[[0, 1], [2, 3]])
    grad = lax.all_gather(grad, "tp", axis=0, tiled=True, axis_index_groups=[[0, 3], [1, 2]])
    (qd,) = run(
        project_kernel, [((ROWS, 2 * WIDTH + MODEL), BF16)], (grad, out_weight, attn_query)
    )
    qd = lax.all_gather(qd, NEAR, axis=0, tiled=False)
    lanes = 2 * NEARS
    stats, *kept = run(
        stats_kernel,
        [((QROWS + 8, WIDTH), F32)]
        + [((NF * slots, lanes * slots), F32) for slots in (CAP2, CAP2, PAD3, PAD3)],
        (limits, kv, qd),
    )
    stats = lax.all_gather(stats, NEAR, axis=0, tiled=False)
    back, dq = run(
        grads_kernel,
        [((NF, BACK, WIDTH), BF16), ((QROWS, WIDTH), F32)],
        (kv, qd, stats, *kept),
    )
    back = lax.all_to_all(back, FAR, 0, 0)
    dq = lax.all_gather(dq, NEAR, axis=0, tiled=False)
    (query_grad,) = run(query_kernel, [((SLOTS, WIDTH), BF16)], (dq,))
    key_grad, value_grad, weight_grad = run(
        last_kernel,
        [((SLOTS, WIDTH), BF16), ((SLOTS, WIDTH), BF16), ((COLS, WIDTH), F32)],
        (back,),
    )
    return query_grad, key_grad, value_grad, weight_grad.T


def solution(mesh):
    grid = Mesh(mesh.devices.reshape(NZ, NY, NX, NC, TP), ("z", "y", "x", "c", "tp"))
    seq = ("z", "y", "x", "c")
    rows = P(seq, "tp")
    return jax.shard_map(
        on_device,
        mesh=grid,
        in_specs=(P(), P(), rows, rows, rows, rows, P("tp", None)),
        out_specs=(rows, rows, rows, P("tp", seq)),
        check_vma=False,
    )
```

```python
import jax
import jax.numpy as jnp
from jax import lax
from jax.experimental import pallas as pl
from jax.experimental.pallas import tpu as pltpu
from jax.sharding import Mesh
from jax.sharding import PartitionSpec as P

HS = 128
NZ, NY, NX, NC = 8, 2, 4, 2
FAR = ("z", "x")
NEAR = ("y", "c")
NF, NEARS = NZ * NX, NY * NC
TP = 4
SLOTS = 20
CAP2 = 16
CAP3 = 4
PAD3 = 8
ROWS = CAP2 + PAD3
WIDTH = 2 * HS
MODEL = 2048
COLS = MODEL // 128
QROWS = NEARS * ROWS
BACK = 2 * CAP2 + PAD3 + COLS
PIECES = 3
STATS = 16
BATCH = 8
SCALE = HS**-0.5
LOW = -1e30
F32 = jnp.float32
BF16 = jnp.bfloat16

NT = (((1,), (1,)), ((), ()))
NN = (((1,), (0,)), ((), ()))
TN = (((0,), (0,)), ((), ()))


def mm(left, right, dims):
    return lax.dot_general(left, right, dims, preferred_element_type=F32)


def split_rows(block):
    wide = block.astype(F32)
    count, _, width = wide.shape
    second = wide[:, :CAP2].reshape(count * CAP2, width).astype(BF16)
    third = wide[:, CAP2:].reshape(count * PAD3, width).astype(BF16)
    return second, third


def by_head(rows):
    column = lax.broadcasted_iota(jnp.int32, rows.shape, 1)
    zero = jnp.zeros_like(rows)
    return jnp.concatenate(
        [jnp.where(column < HS, rows, zero), jnp.where(column < HS, zero, rows)], axis=0
    )


def head_blocks(both):
    count = both.shape[0] // 2
    column = lax.broadcasted_iota(jnp.int32, (count, WIDTH), 1)
    return jnp.where(column < HS, both[:count], both[count:])


def shard_of(z, y, x, c):
    return ((z * NY + y) * NX + x) * NC + c


def place():
    return tuple(lax.axis_index(axis) for axis in ("z", "y", "x", "c"))


def allowed(limit_ref, which, slots):
    z, y, x, c = place()
    shape = (NF * slots, 2 * NEARS * slots)
    key_row = lax.broadcasted_iota(jnp.int32, shape, 0)
    query_row = lax.broadcasted_iota(jnp.int32, shape, 1) % (NEARS * slots)
    key_far, key_slot = key_row // slots, key_row % slots
    key_shard = shard_of(key_far // NX, y, key_far % NX, c)
    near, query_slot = query_row // slots, query_row % slots
    query_shard = shard_of(z, near // NC, x, near % NC)
    limit = limit_ref[which * NF : (which + 1) * NF, : shape[1]]
    limit = jnp.broadcast_to(limit[:, None, :], (NF, slots, shape[1])).reshape(shape)
    in_order = key_shard * slots + key_slot <= query_shard * slots + query_slot
    return in_order & (key_slot < limit)


def blocks(kv_ref, qd_ref):
    kv = kv_ref[...].astype(F32)
    third = kv[:, 2 * CAP2 :]
    shifted = jnp.concatenate([third[:, CAP3:], third[:, :CAP3]], axis=1)
    pairs = ((kv[:, :CAP2], kv[:, CAP2 : 2 * CAP2]), (third, shifted))
    qd_parts = split_rows(qd_ref[:, :, : 2 * WIDTH])
    found = []
    for which, slots in ((0, CAP2), (1, PAD3)):
        key, value = (part.reshape(NF * slots, WIDTH).astype(BF16) for part in pairs[which])
        qd = qd_parts[which]
        found.append((which, slots, key, value, by_head(qd[:, :WIDTH]), by_head(qd[:, WIDTH:])))
    return found


def padded(block):
    rest = jnp.zeros((ROWS - SLOTS, block.shape[1]), F32)
    return jnp.concatenate([block.astype(F32), rest], axis=0).astype(BF16)


def start_kernel(
    counts_any, key_any, value_any, grad_any, kv_any, grad_ref, limit_ref, counts, key, value, grad, block, sems, out_sems
):
    moves = [
        pltpu.make_async_copy(source, target, sems.at[i])
        for i, (source, target) in enumerate(
            ((key_any, key), (value_any, value), (counts_any, counts), (grad_any, grad))
        )
    ]
    for move in moves:
        move.start()
    moves[0].wait()
    moves[1].wait()
    keys, values = key[...].astype(F32), value[...].astype(F32)
    packed = jnp.concatenate(
        [keys[:CAP2], values[:CAP2], keys[CAP2:], values[CAP2:]], axis=0
    ).astype(BF16)
    for i in range(BATCH):
        block[i] = packed
    sends = [
        pltpu.make_async_copy(block, kv_any.at[i * BATCH : (i + 1) * BATCH], out_sems.at[i])
        for i in range(NF // BATCH)
    ]
    for send in sends:
        send.start()
    moves[2].wait()
    moves[3].wait()
    z, y, x, c = place()
    shard = shard_of(z, y, x, c)
    slot = lax.broadcasted_iota(jnp.int32, (SLOTS, 512), 0)
    live = slot < jnp.where(slot < CAP2, counts[0, shard], CAP2 + counts[1, shard])
    grad_ref[...] = jnp.where(live, grad[...].astype(F32), 0.0).astype(BF16)
    for which in range(2):
        for f in range(NF):
            limit = counts[which, shard_of(f // NX, y, f % NX, c)]
            limit_ref[which * NF + f : which * NF + f + 1, :] = jnp.full((1, HS), limit, jnp.int32)
    for send in sends:
        send.wait()


def project_kernel(grad_ref, weight_ref, query_ref, out_ref):
    total = jnp.zeros((SLOTS, WIDTH), F32)
    for t in range(TP):
        piece = grad_ref[t]
        total += mm(piece, weight_ref[:, t * 512 : (t + 1) * 512], NT)
        out_ref[:, 2 * WIDTH + t * 512 : 2 * WIDTH + (t + 1) * 512] = padded(piece)
    out_ref[:, :WIDTH] = padded(query_ref[...])
    out_ref[:, WIDTH : 2 * WIDTH] = padded(total.astype(BF16))


def stats_kernel(limit_ref, kv_ref, qd_ref, out_ref, *kept):
    start = 0
    stats = []
    for which, slots, key, value, query, d_attn in blocks(kv_ref, qd_ref):
        mask = allowed(limit_ref, which, slots)
        scores = jnp.where(mask, mm(key, query, NT) * SCALE, LOW)
        dprob = mm(value, d_attn, NT)
        kept[2 * which][...] = scores
        kept[2 * which + 1][...] = dprob
        top = jnp.max(scores, axis=0, keepdims=True)
        weights = jnp.where(mask, jnp.exp(scores - top), 0.0)
        total = jnp.sum(weights, axis=0, keepdims=True)
        none = total == 0.0
        weights = weights * (1.0 / jnp.where(none, 1.0, total))
        logs = jnp.where(none, LOW, top + jnp.log(jnp.where(none, 1.0, total)))
        delta = jnp.sum(weights * dprob, axis=0, keepdims=True)
        attended = head_blocks(mm(weights.astype(BF16), value, TN))
        out_ref[start : start + NEARS * slots] = attended.astype(BF16)
        start += NEARS * slots
        for row in (logs, delta):
            row = jnp.concatenate([row, jnp.zeros((1, WIDTH - row.shape[1]), F32)], axis=1)
            for _ in range(PIECES):
                piece = row.astype(BF16).astype(F32)
                stats.append(piece)
                row = row - piece
    rest = jnp.zeros((STATS - len(stats), WIDTH), F32)
    out_ref[start:] = jnp.concatenate(stats + [rest], axis=0).astype(BF16)


def grads_kernel(kv_ref, qd_ref, in_ref, *refs):
    kept, (out_ref, dq_ref) = refs[:4], refs[4:]
    _, y, _, c = place()
    lines = in_ref[:, QROWS:].astype(F32)
    attended = []
    d_key, d_value = [], []
    start = 0
    for which, slots, key, _, query, d_attn in blocks(kv_ref, qd_ref):
        count = NEARS * slots
        logs, deltas = (
            jnp.sum(lines[:, first : first + PIECES, : 2 * count], axis=1)
            for first in (2 * which * PIECES, (2 * which + 1) * PIECES)
        )
        top = jnp.max(logs, axis=0, keepdims=True)
        log_total = top + jnp.log(jnp.sum(jnp.exp(logs - top), axis=0, keepdims=True))
        share = jnp.exp(logs - log_total)
        delta = jnp.sum(share * deltas, axis=0, keepdims=True)
        share_down = jnp.concatenate([share, jnp.zeros((8 - NEARS, 2 * count), F32)], axis=0).T
        column = lax.broadcasted_iota(jnp.int32, (count, WIDTH), 1)
        total = jnp.zeros((count, WIDTH), F32)
        for n in range(NEARS):
            own = jnp.where(column < HS, share_down[:count, n : n + 1], share_down[count:, n : n + 1])
            total += own * in_ref[n, start : start + count].astype(F32)
        attended.append(total)

        prob = jnp.exp(kept[2 * which][...] - log_total)
        dscore = (prob * (kept[2 * which + 1][...] - delta)).astype(BF16)
        d_value.append(mm(prob.astype(BF16), d_attn, NN).reshape(NF, slots, WIDTH))
        d_key.append((mm(dscore, query, NN) * SCALE).reshape(NF, slots, WIDTH))
        dq_ref[start : start + count] = head_blocks(mm(dscore, key, TN)) * SCALE
        start += count
    out_ref[:, :CAP2] = d_key[0].astype(BF16)
    out_ref[:, CAP2 : 2 * CAP2] = d_value[0].astype(BF16)
    attended = jnp.concatenate(attended, axis=0).astype(BF16)
    parts = []
    for z in range(NZ):
        column = pl.multiple_of(2 * WIDTH + (z * NY + y) * HS, HS)
        second, third = split_rows(qd_ref[:, :, pl.ds(column, HS)])
        grad = jnp.concatenate([second, third], axis=0)
        parts.append(mm(grad, attended, TN).reshape(NX, NC, COLS, WIDTH))
    parts = jnp.concatenate(parts, axis=0)
    own = jnp.where(c == 0, parts[:, 0], parts[:, 1])
    third = jnp.concatenate([d_key[1][:, :CAP3], d_value[1][:, :CAP3]], axis=1)
    out_ref[:, 2 * CAP2 :] = jnp.concatenate([third, own], axis=1).astype(BF16)


def query_kernel(in_ref, dq_ref):
    _, y, _, c = place()
    near = y * NC + c
    second = pl.ds(pl.multiple_of(near * CAP2, CAP2), CAP2)
    third = pl.ds(pl.multiple_of(NEARS * CAP2 + near * PAD3, PAD3), PAD3)
    total = jnp.concatenate(
        [jnp.sum(in_ref[:, second, :], axis=0), jnp.sum(in_ref[:, third, :], axis=0)[:CAP3]], axis=0
    )
    dq_ref[...] = total.astype(BF16)


def last_kernel(in_ref, dk_ref, dv_ref, dw_ref):
    total = jnp.sum(in_ref[...].astype(F32), axis=0)
    third = 2 * CAP2
    dk_ref[...] = jnp.concatenate([total[:CAP2], total[third : third + CAP3]], axis=0).astype(BF16)
    dv_ref[...] = jnp.concatenate(
        [total[CAP2 : 2 * CAP2], total[third + CAP3 : third + 2 * CAP3]], axis=0
    ).astype(BF16)
    dw_ref[...] = total[third + PAD3 :]


def on_device(token_picks, live_counts, attn_query, attn_key, attn_value, out_grad, out_weight):
    del token_picks
    vmem = pl.BlockSpec(memory_space=pltpu.VMEM)
    anywhere = pl.BlockSpec(memory_space=pl.ANY)
    parameters = pltpu.CompilerParams(vmem_limit_bytes=32 * 2**20)

    def run(kernel, outs, args):
        return pl.pallas_call(
            kernel,
            out_shape=[jax.ShapeDtypeStruct(*o) for o in outs],
            in_specs=[vmem] * len(args),
            out_specs=[vmem] * len(outs),
            compiler_params=parameters,
        )(*args)

    live_counts = live_counts.T
    kv, out_grad, limits = pl.pallas_call(
        start_kernel,
        out_shape=[
            jax.ShapeDtypeStruct((NF, 2 * SLOTS, WIDTH), BF16),
            jax.ShapeDtypeStruct(out_grad.shape, BF16),
            jax.ShapeDtypeStruct((2 * NF, HS), jnp.int32),
        ],
        in_specs=[anywhere] * 4,
        out_specs=[anywhere, vmem, vmem],
        scratch_shapes=[
            pltpu.SMEM(live_counts.shape, jnp.int32),
            pltpu.VMEM((SLOTS, WIDTH), BF16),
            pltpu.VMEM((SLOTS, WIDTH), BF16),
            pltpu.VMEM(out_grad.shape, BF16),
            pltpu.VMEM((BATCH, 2 * SLOTS, WIDTH), BF16),
            pltpu.SemaphoreType.DMA((4,)),
            pltpu.SemaphoreType.DMA((NF // BATCH,)),
        ],
    )(live_counts, attn_key, attn_value, out_grad)
    kv = lax.all_to_all(kv, FAR, 0, 0)
    grad = lax.all_gather(out_grad[None], "tp", axis=0, tiled=True, axis_index_groups=[[0, 1], [2, 3]])
    grad = lax.all_gather(grad, "tp", axis=0, tiled=True, axis_index_groups=[[0, 3], [1, 2]])
    (qd,) = run(
        project_kernel, [((ROWS, 2 * WIDTH + MODEL), BF16)], (grad, out_weight, attn_query)
    )
    qd = lax.all_gather(qd, NEAR, axis=0, tiled=False)
    lanes = 2 * NEARS
    stats, *kept = run(
        stats_kernel,
        [((QROWS + STATS, WIDTH), BF16)]
        + [((NF * slots, lanes * slots), F32) for slots in (CAP2, CAP2, PAD3, PAD3)],
        (limits, kv, qd),
    )
    stats = lax.all_gather(stats, NEAR, axis=0, tiled=False)
    back, dq = run(
        grads_kernel,
        [((NF, BACK, WIDTH), BF16), ((QROWS, WIDTH), F32)],
        (kv, qd, stats, *kept),
    )
    back = lax.all_to_all(back, FAR, 0, 0)
    dq = lax.all_gather(dq, NEAR, axis=0, tiled=False)
    (query_grad,) = run(query_kernel, [((SLOTS, WIDTH), BF16)], (dq,))
    key_grad, value_grad, weight_grad = run(
        last_kernel,
        [((SLOTS, WIDTH), BF16), ((SLOTS, WIDTH), BF16), ((COLS, WIDTH), F32)],
        (back,),
    )
    return query_grad, key_grad, value_grad, weight_grad.T


def solution(mesh):
    grid = Mesh(mesh.devices.reshape(NZ, NY, NX, NC, TP), ("z", "y", "x", "c", "tp"))
    seq = ("z", "y", "x", "c")
    rows = P(seq, "tp")
    return jax.shard_map(
        on_device,
        mesh=grid,
        in_specs=(P(), P(), rows, rows, rows, rows, P("tp", None)),
        out_specs=(rows, rows, rows, P("tp", seq)),
        check_vma=False,
    )
```

```python
import jax
import jax.numpy as jnp
from jax import lax
from jax.experimental import pallas as pl
from jax.experimental.pallas import tpu as pltpu
from jax.sharding import Mesh
from jax.sharding import PartitionSpec as P

HS = 128
NZ, NY, NX, NC = 8, 2, 4, 2
FAR = ("z", "x")
NEAR = ("y", "c")
NF, NEARS = NZ * NX, NY * NC
TP = 4
SLOTS = 20
CAP2 = 16
CAP3 = 4
PAD3 = 8
ROWS = CAP2 + PAD3
WIDTH = 2 * HS
MODEL = 2048
COLS = MODEL // 128
QROWS = NEARS * ROWS
BACK = 2 * CAP2 + PAD3 + COLS
PIECES = 3
STATS = 16
PART = 8
BATCH = 8
SCALE = HS**-0.5
LOW = -1e30
F32 = jnp.float32
BF16 = jnp.bfloat16

NT = (((1,), (1,)), ((), ()))
NN = (((1,), (0,)), ((), ()))
TN = (((0,), (0,)), ((), ()))


def mm(left, right, dims):
    return lax.dot_general(left, right, dims, preferred_element_type=F32)


def split_rows(block):
    wide = block.astype(F32)
    count, _, width = wide.shape
    second = wide[:, :CAP2].reshape(count * CAP2, width).astype(BF16)
    third = wide[:, CAP2:].reshape(count * PAD3, width).astype(BF16)
    return second, third


def by_head(rows):
    column = lax.broadcasted_iota(jnp.int32, rows.shape, 1)
    zero = jnp.zeros_like(rows)
    return jnp.concatenate(
        [jnp.where(column < HS, rows, zero), jnp.where(column < HS, zero, rows)], axis=0
    )


def head_blocks(both):
    count = both.shape[0] // 2
    column = lax.broadcasted_iota(jnp.int32, (count, WIDTH), 1)
    return jnp.where(column < HS, both[:count], both[count:])


def shard_of(z, y, x, c):
    return ((z * NY + y) * NX + x) * NC + c


def place():
    return tuple(lax.axis_index(axis) for axis in ("z", "y", "x", "c"))


def allowed(limit_ref, which, slots):
    z, y, x, c = place()
    shape = (NF * slots, 2 * NEARS * slots)
    key_row = lax.broadcasted_iota(jnp.int32, shape, 0)
    query_row = lax.broadcasted_iota(jnp.int32, shape, 1) % (NEARS * slots)
    key_far, key_slot = key_row // slots, key_row % slots
    key_shard = shard_of(key_far // NX, y, key_far % NX, c)
    near, query_slot = query_row // slots, query_row % slots
    query_shard = shard_of(z, near // NC, x, near % NC)
    limit = limit_ref[which * NF : (which + 1) * NF, : shape[1]]
    limit = jnp.broadcast_to(limit[:, None, :], (NF, slots, shape[1])).reshape(shape)
    in_order = key_shard * slots + key_slot <= query_shard * slots + query_slot
    return in_order & (key_slot < limit)


def padded(block):
    rest = jnp.zeros((ROWS - SLOTS, block.shape[1]), F32)
    return jnp.concatenate([block.astype(F32), rest], axis=0).astype(BF16)


def start_kernel(
    counts_any, key_any, value_any, kv_any, live_any, limit_any, counts, key, value, block, live, limits, sems, out_sems
):
    moves = [
        pltpu.make_async_copy(source, target, sems.at[i])
        for i, (source, target) in enumerate(((key_any, key), (value_any, value), (counts_any, counts)))
    ]
    for move in moves:
        move.start()
    moves[0].wait()
    moves[1].wait()
    keys, values = key[...].astype(F32), value[...].astype(F32)
    packed = jnp.concatenate(
        [keys[:CAP2], values[:CAP2], keys[CAP2:], values[CAP2:]], axis=0
    ).astype(BF16)
    for i in range(BATCH):
        block[i] = packed
    batches = NF // BATCH
    sends = [
        pltpu.make_async_copy(block, kv_any.at[i * BATCH : (i + 1) * BATCH], out_sems.at[i])
        for i in range(batches)
    ]
    for send in sends:
        send.start()
    moves[2].wait()
    z, y, x, c = place()
    shard = shard_of(z, y, x, c)
    slot = lax.broadcasted_iota(jnp.int32, live.shape, 0)
    limit = jnp.where(slot < CAP2, counts[0, shard], CAP2 + counts[1, shard])
    live[...] = jnp.where(slot < limit, 1.0, 0.0)
    for which in range(2):
        for f in range(NF):
            limit = counts[which, shard_of(f // NX, y, f % NX, c)]
            limits[which * NF + f : which * NF + f + 1, :] = jnp.full((1, HS), limit, jnp.int32)
    rest = [
        pltpu.make_async_copy(live, live_any, out_sems.at[batches]),
        pltpu.make_async_copy(limits, limit_any, out_sems.at[batches + 1]),
    ]
    for send in rest:
        send.start()
    for send in sends + rest:
        send.wait()


def pair_kernel(own_ref, other_ref, out_ref):
    out_ref[0] = own_ref[...]
    out_ref[1] = other_ref[...]


def project_kernel(live_ref, grad_ref, weight_ref, query_ref, out_ref):
    me = lax.axis_index("tp")
    outer = (me == 0) | (me == 3)
    first, second = jnp.where(outer, 0, 1), jnp.where(outer, 3, 2)
    live = live_ref[:, :1]
    total = jnp.zeros((ROWS, WIDTH), F32)
    for k, t in enumerate((first, 1 - first, second, 5 - second)):
        column = pl.multiple_of(t * 512, 512)
        wide = jnp.concatenate(
            [grad_ref[k].astype(F32), jnp.zeros((ROWS - SLOTS, 512), F32)], axis=0
        )
        piece = (wide * live).astype(BF16)
        total += mm(piece, weight_ref[:, pl.ds(column, 512)], NT)
        out_ref[:, pl.ds(2 * WIDTH + column, 512)] = piece
    out_ref[:, :WIDTH] = padded(query_ref[...])
    out_ref[:, WIDTH : 2 * WIDTH] = total.astype(BF16)


def prepare_kernel(limit_ref, qd_ref, *refs):
    _, y, _, c = place()
    qd_parts = split_rows(qd_ref[:, :, : 2 * WIDTH])
    for which, slots in ((0, CAP2), (1, PAD3)):
        query_ref, d_attn_ref, bias_ref = refs[3 * which : 3 * which + 3]
        query_ref[...] = by_head(qd_parts[which][:, :WIDTH])
        d_attn_ref[...] = by_head(qd_parts[which][:, WIDTH:])
        bias_ref[...] = jnp.where(allowed(limit_ref, which, slots), 0.0, LOW)
    columns_ref = refs[6]
    for z in range(NZ):
        column = pl.multiple_of(2 * WIDTH + (z * NY + y) * HS, HS)
        wide = qd_ref[:, :, pl.ds(column, HS)].astype(F32)
        rows = jnp.concatenate(
            [wide[:, :CAP2].reshape(NEARS * CAP2, HS), wide[:, CAP2:].reshape(NEARS * PAD3, HS)], axis=0
        )
        down = rows.T.reshape(NX, NC, COLS, QROWS)
        own = jnp.where(c == 0, down[:, 0], down[:, 1]).reshape(NX * COLS, QROWS)
        columns_ref[z * NX * COLS : (z + 1) * NX * COLS] = own.astype(BF16)


def unpacked(kv_ref):
    third = kv_ref[:, 2 * CAP2 :].astype(F32)
    shifted = jnp.concatenate([third[:, CAP3:], third[:, :CAP3]], axis=1)
    second = (kv_ref[:, :CAP2].reshape(NF * CAP2, WIDTH), kv_ref[:, CAP2 : 2 * CAP2].reshape(NF * CAP2, WIDTH))
    return (second, tuple(part.reshape(NF * PAD3, WIDTH).astype(BF16) for part in (third, shifted)))


def stats_kernel(kv_ref, *refs):
    ready, out_ref, kept = refs[:6], refs[6], refs[7:]
    kv = unpacked(kv_ref)
    start = 0
    stats = []
    for which, slots in ((0, CAP2), (1, PAD3)):
        key, value = kv[which]
        query, d_attn, bias = (ref[...] for ref in ready[3 * which : 3 * which + 3])
        scores = mm(key, query, NT) * SCALE + bias
        dprob = mm(value, d_attn, NT)
        kept[2 * which][...] = scores
        kept[2 * which + 1][...] = dprob
        top = jnp.max(scores, axis=0, keepdims=True)
        weights = jnp.exp(scores - top)
        total = jnp.sum(weights, axis=0, keepdims=True)
        weights = weights * (1.0 / total)
        logs = jnp.where(top < 0.5 * LOW, LOW, top + jnp.log(total))
        delta = jnp.sum(weights * dprob, axis=0, keepdims=True)
        attended = head_blocks(mm(weights.astype(BF16), value, TN))
        out_ref[start : start + NEARS * slots] = attended.astype(BF16)
        start += NEARS * slots
        for row in (logs, delta):
            row = jnp.concatenate([row, jnp.zeros((1, WIDTH - row.shape[1]), F32)], axis=1)
            for _ in range(PIECES):
                piece = row.astype(BF16).astype(F32)
                stats.append(piece)
                row = row - piece
    rest = jnp.zeros((STATS - len(stats), WIDTH), F32)
    out_ref[start:] = jnp.concatenate(stats + [rest], axis=0).astype(BF16)


def grads_kernel(in_ref, *refs):
    ready, columns_ref, kept, out_any, dscore_refs = refs[:4], refs[4], refs[5:9], refs[9], refs[10:12]
    block, sems = refs[12:]
    lines = in_ref[:, QROWS:].astype(F32)
    attended, totals = [], []
    start = 0
    for which, slots in ((0, CAP2), (1, PAD3)):
        count = NEARS * slots
        logs, deltas = (
            jnp.sum(lines[:, first : first + PIECES, : 2 * count], axis=1)
            for first in (2 * which * PIECES, (2 * which + 1) * PIECES)
        )
        top = jnp.max(logs, axis=0, keepdims=True)
        log_total = top + jnp.log(jnp.sum(jnp.exp(logs - top), axis=0, keepdims=True))
        share = jnp.exp(logs - log_total)
        totals.append((log_total, jnp.sum(share * deltas, axis=0, keepdims=True)))
        share_down = jnp.concatenate([share, jnp.zeros((8 - NEARS, 2 * count), F32)], axis=0).T
        column = lax.broadcasted_iota(jnp.int32, (count, WIDTH), 1)
        total = jnp.zeros((count, WIDTH), F32)
        for n in range(NEARS):
            own = jnp.where(column < HS, share_down[:count, n : n + 1], share_down[count:, n : n + 1])
            total += own * in_ref[n, start : start + count].astype(F32)
        attended.append(total)
        start += count
    attended = jnp.concatenate(attended, axis=0).astype(BF16)

    sends = []
    for i in range(NF // PART):
        parts = slice(i * PART, (i + 1) * PART)
        third = []
        for which, slots in ((0, CAP2), (1, PAD3)):
            query, d_attn = (ref[...] for ref in ready[2 * which : 2 * which + 2])
            log_total, delta = totals[which]
            keys = slice(i * PART * slots, (i + 1) * PART * slots)
            prob = jnp.exp(kept[2 * which][keys] - log_total)
            dscore = (prob * (kept[2 * which + 1][keys] - delta)).astype(BF16)
            dscore_refs[which][keys] = dscore
            d_key = (mm(dscore, query, NN) * SCALE).reshape(PART, slots, WIDTH)
            d_value = mm(prob.astype(BF16), d_attn, NN).reshape(PART, slots, WIDTH)
            if which == 0:
                block[parts, :CAP2] = d_key.astype(BF16)
                block[parts, CAP2 : 2 * CAP2] = d_value.astype(BF16)
            else:
                third = [d_key[:, :CAP3], d_value[:, :CAP3]]
        columns = columns_ref[i * PART * COLS : (i + 1) * PART * COLS]
        own = mm(columns, attended, NN).reshape(PART, COLS, WIDTH)
        block[parts, 2 * CAP2 :] = jnp.concatenate([*third, own], axis=1).astype(BF16)
        sends.append(pltpu.make_async_copy(block.at[parts], out_any.at[parts], sems.at[i]))
        sends[-1].start()
    for send in sends:
        send.wait()


def partial_kernel(kv_ref, dscore2_ref, dscore3_ref, out_ref):
    start = 0
    for (key, _), dscore_ref in zip(unpacked(kv_ref), (dscore2_ref, dscore3_ref)):
        count = dscore_ref.shape[1] // 2
        out_ref[start : start + count] = head_blocks(mm(dscore_ref[...], key, TN)) * SCALE
        start += count


def query_kernel(in_ref, dq_ref):
    _, y, _, c = place()
    near = y * NC + c
    second = pl.ds(pl.multiple_of(near * CAP2, CAP2), CAP2)
    third = pl.ds(pl.multiple_of(NEARS * CAP2 + near * PAD3, PAD3), PAD3)
    total = jnp.concatenate(
        [jnp.sum(in_ref[:, second, :], axis=0), jnp.sum(in_ref[:, third, :], axis=0)[:CAP3]], axis=0
    )
    dq_ref[...] = total.astype(BF16)


def last_kernel(in_ref, dk_ref, dv_ref, dw_ref):
    total = jnp.sum(in_ref[...].astype(F32), axis=0)
    third = 2 * CAP2
    dk_ref[...] = jnp.concatenate([total[:CAP2], total[third : third + CAP3]], axis=0).astype(BF16)
    dv_ref[...] = jnp.concatenate(
        [total[CAP2 : 2 * CAP2], total[third + CAP3 : third + 2 * CAP3]], axis=0
    ).astype(BF16)
    dw_ref[...] = total[third + PAD3 :]


def on_device(token_picks, live_counts, attn_query, attn_key, attn_value, out_grad, out_weight):
    del token_picks
    vmem = pl.BlockSpec(memory_space=pltpu.VMEM)
    anywhere = pl.BlockSpec(memory_space=pl.ANY)
    parameters = pltpu.CompilerParams(vmem_limit_bytes=32 * 2**20)

    def run(kernel, outs, args):
        return pl.pallas_call(
            kernel,
            out_shape=[jax.ShapeDtypeStruct(*o) for o in outs],
            in_specs=[vmem] * len(args),
            out_specs=[vmem] * len(outs),
            compiler_params=parameters,
        )(*args)

    live_counts = live_counts.T
    other = lax.ppermute(out_grad, "tp", [(0, 1), (1, 0), (2, 3), (3, 2)])
    kv, live, limits = pl.pallas_call(
        start_kernel,
        out_shape=[
            jax.ShapeDtypeStruct((NF, 2 * SLOTS, WIDTH), BF16),
            jax.ShapeDtypeStruct((ROWS, HS), F32),
            jax.ShapeDtypeStruct((2 * NF, HS), jnp.int32),
        ],
        in_specs=[anywhere] * 3,
        out_specs=[anywhere] * 3,
        scratch_shapes=[
            pltpu.SMEM(live_counts.shape, jnp.int32),
            pltpu.VMEM((SLOTS, WIDTH), BF16),
            pltpu.VMEM((SLOTS, WIDTH), BF16),
            pltpu.VMEM((BATCH, 2 * SLOTS, WIDTH), BF16),
            pltpu.VMEM((ROWS, HS), F32),
            pltpu.VMEM((2 * NF, HS), jnp.int32),
            pltpu.SemaphoreType.DMA((3,)),
            pltpu.SemaphoreType.DMA((NF // BATCH + 2,)),
        ],
    )(live_counts, attn_key, attn_value)
    kv = lax.all_to_all(kv, FAR, 0, 0)
    (grad,) = pl.pallas_call(
        pair_kernel,
        out_shape=[jax.ShapeDtypeStruct((2, *out_grad.shape), BF16)],
        in_specs=[vmem] * 2,
        out_specs=[vmem],
        compiler_params=parameters,
        cost_estimate=pl.CostEstimate(flops=10**11, bytes_accessed=10**8, transcendentals=0),
    )(out_grad, other)
    grad = lax.all_gather(grad, "tp", axis=0, tiled=True, axis_index_groups=[[0, 3], [1, 2]])
    (qd,) = run(
        project_kernel, [((ROWS, 2 * WIDTH + MODEL), BF16)], (live, grad, out_weight, attn_query)
    )
    qd = lax.all_gather(qd, NEAR, axis=0, tiled=False)
    kinds = (CAP2, PAD3)
    tables = [(NF * slots, 2 * NEARS * slots) for slots in kinds]
    *ready, columns = run(
        prepare_kernel,
        [
            item
            for table in tables
            for item in (((table[1], WIDTH), BF16), ((table[1], WIDTH), BF16), (table, F32))
        ]
        + [((NF * COLS, QROWS), BF16)],
        (limits, qd),
    )
    stats, *kept = run(
        stats_kernel,
        [((QROWS + STATS, WIDTH), BF16)] + [(table, F32) for table in tables for _ in range(2)],
        (kv, *ready),
    )
    stats = lax.all_gather(stats, NEAR, axis=0, tiled=False)
    back, *dscores = pl.pallas_call(
        grads_kernel,
        out_shape=[jax.ShapeDtypeStruct((NF, BACK, WIDTH), BF16)]
        + [jax.ShapeDtypeStruct(table, BF16) for table in tables],
        in_specs=[vmem] * 10,
        out_specs=[anywhere, vmem, vmem],
        scratch_shapes=[pltpu.VMEM((NF, BACK, WIDTH), BF16), pltpu.SemaphoreType.DMA((NF // PART,))],
        compiler_params=parameters,
    )(stats, *ready[0:2], *ready[3:5], columns, *kept)
    back = lax.all_to_all(back, FAR, 0, 0)
    (dq,) = run(partial_kernel, [((QROWS, WIDTH), F32)], (kv, *dscores))
    dq = lax.all_gather(dq, NEAR, axis=0, tiled=False)
    (query_grad,) = run(query_kernel, [((SLOTS, WIDTH), BF16)], (dq,))
    key_grad, value_grad, weight_grad = run(
        last_kernel,
        [((SLOTS, WIDTH), BF16), ((SLOTS, WIDTH), BF16), ((COLS, WIDTH), F32)],
        (back,),
    )
    return query_grad, key_grad, value_grad, weight_grad.T


def solution(mesh):
    grid = Mesh(mesh.devices.reshape(NZ, NY, NX, NC, TP), ("z", "y", "x", "c", "tp"))
    seq = ("z", "y", "x", "c")
    rows = P(seq, "tp")
    return jax.shard_map(
        on_device,
        mesh=grid,
        in_specs=(P(), P(), rows, rows, rows, rows, P("tp", None)),
        out_specs=(rows, rows, rows, P("tp", seq)),
        check_vma=False,
    )
```

```python
import jax
import jax.numpy as jnp
from jax import lax
from jax.experimental import pallas as pl
from jax.experimental.pallas import tpu as pltpu
from jax.sharding import PartitionSpec as P

HS = 128
NZ, NY, NX, NC = 8, 2, 4, 2
NF, NEARS = NZ * NX, NY * NC
TP = 4
SLOTS = 20
CAP2 = 16
CAP3 = 4
PAD3 = 8
ROWS = CAP2 + PAD3
WIDTH = 2 * HS
MODEL = 2048
COLS = MODEL // 128
QROWS = NEARS * ROWS
BACK = 2 * CAP2 + PAD3 + COLS
PIECES = 3
STATS = 16
PART = 8
BATCH = 8
SCALE = HS**-0.5
LOW = -1e30
F32 = jnp.float32
BF16 = jnp.bfloat16

NT = (((1,), (1,)), ((), ()))
NN = (((1,), (0,)), ((), ()))
TN = (((0,), (0,)), ((), ()))


def mm(left, right, dims):
    return lax.dot_general(left, right, dims, preferred_element_type=F32)


def split_rows(block):
    wide = block.astype(F32)
    count, _, width = wide.shape
    second = wide[:, :CAP2].reshape(count * CAP2, width).astype(BF16)
    third = wide[:, CAP2:].reshape(count * PAD3, width).astype(BF16)
    return second, third


def by_head(rows):
    column = lax.broadcasted_iota(jnp.int32, rows.shape, 1)
    zero = jnp.zeros_like(rows)
    return jnp.concatenate(
        [jnp.where(column < HS, rows, zero), jnp.where(column < HS, zero, rows)], axis=0
    )


def head_blocks(both):
    count = both.shape[0] // 2
    column = lax.broadcasted_iota(jnp.int32, (count, WIDTH), 1)
    return jnp.where(column < HS, both[:count], both[count:])


def shard_of(z, y, x, c):
    return ((z * NY + y) * NX + x) * NC + c


def place():
    index = lax.axis_index("seq")
    return index // (NY * NX * NC), index // (NX * NC) % NY, index // NC % NX, index % NC


def far_place(index):
    return NZ - 1 - index // NX, index % NX


def far_groups():
    return [
        [shard_of(far_place(f)[0], y, far_place(f)[1], c) for f in range(NF)]
        for y in range(NY)
        for c in range(NC)
    ]


def near_groups():
    return [
        [shard_of(z, n // NC, x, n % NC) for n in range(NEARS)] for z in range(NZ) for x in range(NX)
    ]


def allowed(limit_ref, which, slots):
    z, y, x, c = place()
    shape = (NF * slots, 2 * NEARS * slots)
    key_row = lax.broadcasted_iota(jnp.int32, shape, 0)
    query_row = lax.broadcasted_iota(jnp.int32, shape, 1) % (NEARS * slots)
    key_far, key_slot = key_row // slots, key_row % slots
    key_z, key_x = far_place(key_far)
    key_shard = shard_of(key_z, y, key_x, c)
    near, query_slot = query_row // slots, query_row % slots
    query_shard = shard_of(z, near // NC, x, near % NC)
    limit = limit_ref[which * NF : (which + 1) * NF, : shape[1]]
    limit = jnp.broadcast_to(limit[:, None, :], (NF, slots, shape[1])).reshape(shape)
    in_order = key_shard * slots + key_slot <= query_shard * slots + query_slot
    return in_order & (key_slot < limit)


def padded(block):
    rest = jnp.zeros((ROWS - SLOTS, block.shape[1]), F32)
    return jnp.concatenate([block.astype(F32), rest], axis=0).astype(BF16)


def start_kernel(
    counts_any, key_any, value_any, kv_any, live_any, limit_any, counts, key, value, block, live, limits, sems, out_sems
):
    moves = [
        pltpu.make_async_copy(source, target, sems.at[i])
        for i, (source, target) in enumerate(((key_any, key), (value_any, value), (counts_any, counts)))
    ]
    for move in moves:
        move.start()
    moves[0].wait()
    moves[1].wait()
    keys, values = key[...].astype(F32), value[...].astype(F32)
    packed = jnp.concatenate(
        [keys[:CAP2], values[:CAP2], keys[CAP2:], values[CAP2:]], axis=0
    ).astype(BF16)
    for i in range(BATCH):
        block[i] = packed
    batches = NF // BATCH
    sends = [
        pltpu.make_async_copy(block, kv_any.at[i * BATCH : (i + 1) * BATCH], out_sems.at[i])
        for i in range(batches)
    ]
    for send in sends:
        send.start()
    moves[2].wait()
    z, y, x, c = place()
    shard = shard_of(z, y, x, c)
    slot = lax.broadcasted_iota(jnp.int32, live.shape, 0)
    limit = jnp.where(slot < CAP2, counts[0, shard], CAP2 + counts[1, shard])
    live[...] = jnp.where(slot < limit, 1.0, 0.0)
    for which in range(2):
        for f in range(NF):
            far_z, far_x = far_place(f)
            limit = counts[which, shard_of(far_z, y, far_x, c)]
            limits[which * NF + f : which * NF + f + 1, :] = jnp.full((1, HS), limit, jnp.int32)
    rest = [
        pltpu.make_async_copy(live, live_any, out_sems.at[batches]),
        pltpu.make_async_copy(limits, limit_any, out_sems.at[batches + 1]),
    ]
    for send in rest:
        send.start()
    for send in sends + rest:
        send.wait()


def pair_kernel(own_ref, other_ref, out_ref):
    out_ref[0] = own_ref[...]
    out_ref[1] = other_ref[...]


def project_kernel(live_ref, grad_ref, weight_ref, query_ref, out_ref):
    me = lax.axis_index("tp")
    outer = (me == 0) | (me == 3)
    first, second = jnp.where(outer, 0, 1), jnp.where(outer, 3, 2)
    live = live_ref[:, :1]
    total = jnp.zeros((ROWS, WIDTH), F32)
    for k, t in enumerate((first, 1 - first, second, 5 - second)):
        column = pl.multiple_of(t * 512, 512)
        wide = jnp.concatenate(
            [grad_ref[k].astype(F32), jnp.zeros((ROWS - SLOTS, 512), F32)], axis=0
        )
        piece = (wide * live).astype(BF16)
        total += mm(piece, weight_ref[:, pl.ds(column, 512)], NT)
        out_ref[:, pl.ds(2 * WIDTH + column, 512)] = piece
    out_ref[:, :WIDTH] = padded(query_ref[...])
    out_ref[:, WIDTH : 2 * WIDTH] = total.astype(BF16)


def prepare_kernel(limit_ref, qd_ref, *refs):
    _, y, _, c = place()
    qd_parts = split_rows(qd_ref[:, :, : 2 * WIDTH])
    for which, slots in ((0, CAP2), (1, PAD3)):
        query_ref, d_attn_ref, bias_ref = refs[3 * which : 3 * which + 3]
        query_ref[...] = by_head(qd_parts[which][:, :WIDTH])
        d_attn_ref[...] = by_head(qd_parts[which][:, WIDTH:])
        bias_ref[...] = jnp.where(allowed(limit_ref, which, slots), 0.0, LOW)
    columns_ref = refs[6]
    for step in range(NZ):
        z, _ = far_place(step * NX)
        column = pl.multiple_of(2 * WIDTH + (z * NY + y) * HS, HS)
        wide = qd_ref[:, :, pl.ds(column, HS)].astype(F32)
        rows = jnp.concatenate(
            [wide[:, :CAP2].reshape(NEARS * CAP2, HS), wide[:, CAP2:].reshape(NEARS * PAD3, HS)], axis=0
        )
        down = rows.T.reshape(NX, NC, COLS, QROWS)
        own = jnp.where(c == 0, down[:, 0], down[:, 1]).reshape(NX * COLS, QROWS)
        columns_ref[step * NX * COLS : (step + 1) * NX * COLS] = own.astype(BF16)


def unpacked(kv_ref):
    third = kv_ref[:, 2 * CAP2 :].astype(F32)
    shifted = jnp.concatenate([third[:, CAP3:], third[:, :CAP3]], axis=1)
    second = (kv_ref[:, :CAP2].reshape(NF * CAP2, WIDTH), kv_ref[:, CAP2 : 2 * CAP2].reshape(NF * CAP2, WIDTH))
    return (second, tuple(part.reshape(NF * PAD3, WIDTH).astype(BF16) for part in (third, shifted)))


def stats_kernel(kv_ref, *refs):
    ready, out_ref, kept = refs[:6], refs[6], refs[7:]
    kv = unpacked(kv_ref)
    start = 0
    stats = []
    for which, slots in ((0, CAP2), (1, PAD3)):
        key, value = kv[which]
        query, d_attn, bias = (ref[...] for ref in ready[3 * which : 3 * which + 3])
        scores = mm(key, query, NT) * SCALE + bias
        dprob = mm(value, d_attn, NT)
        kept[2 * which][...] = scores
        kept[2 * which + 1][...] = dprob
        top = jnp.max(scores, axis=0, keepdims=True)
        weights = jnp.exp(scores - top)
        total = jnp.sum(weights, axis=0, keepdims=True)
        weights = weights * (1.0 / total)
        logs = jnp.where(top < 0.5 * LOW, LOW, top + jnp.log(total))
        delta = jnp.sum(weights * dprob, axis=0, keepdims=True)
        attended = head_blocks(mm(weights.astype(BF16), value, TN))
        out_ref[start : start + NEARS * slots] = attended.astype(BF16)
        start += NEARS * slots
        for row in (logs, delta):
            row = jnp.concatenate([row, jnp.zeros((1, WIDTH - row.shape[1]), F32)], axis=1)
            for _ in range(PIECES):
                piece = row.astype(BF16).astype(F32)
                stats.append(piece)
                row = row - piece
    rest = jnp.zeros((STATS - len(stats), WIDTH), F32)
    out_ref[start:] = jnp.concatenate(stats + [rest], axis=0).astype(BF16)


def grads_kernel(in_ref, *refs):
    ready, columns_ref, kept, out_any, dscore_refs = refs[:4], refs[4], refs[5:9], refs[9], refs[10:12]
    block, sems = refs[12:]
    lines = in_ref[:, QROWS:].astype(F32)
    attended, totals = [], []
    start = 0
    for which, slots in ((0, CAP2), (1, PAD3)):
        count = NEARS * slots
        logs, deltas = (
            jnp.sum(lines[:, first : first + PIECES, : 2 * count], axis=1)
            for first in (2 * which * PIECES, (2 * which + 1) * PIECES)
        )
        top = jnp.max(logs, axis=0, keepdims=True)
        log_total = top + jnp.log(jnp.sum(jnp.exp(logs - top), axis=0, keepdims=True))
        share = jnp.exp(logs - log_total)
        totals.append((log_total, jnp.sum(share * deltas, axis=0, keepdims=True)))
        share_down = jnp.concatenate([share, jnp.zeros((8 - NEARS, 2 * count), F32)], axis=0).T
        column = lax.broadcasted_iota(jnp.int32, (count, WIDTH), 1)
        total = jnp.zeros((count, WIDTH), F32)
        for n in range(NEARS):
            own = jnp.where(column < HS, share_down[:count, n : n + 1], share_down[count:, n : n + 1])
            total += own * in_ref[n, start : start + count].astype(F32)
        attended.append(total)
        start += count
    attended = jnp.concatenate(attended, axis=0).astype(BF16)

    sends = []
    for i in range(NF // PART):
        parts = slice(i * PART, (i + 1) * PART)
        third = []
        for which, slots in ((0, CAP2), (1, PAD3)):
            query, d_attn = (ref[...] for ref in ready[2 * which : 2 * which + 2])
            log_total, delta = totals[which]
            keys = slice(i * PART * slots, (i + 1) * PART * slots)
            prob = jnp.exp(kept[2 * which][keys] - log_total)
            dscore = (prob * (kept[2 * which + 1][keys] - delta)).astype(BF16)
            dscore_refs[which][keys] = dscore
            d_key = (mm(dscore, query, NN) * SCALE).reshape(PART, slots, WIDTH)
            d_value = mm(prob.astype(BF16), d_attn, NN).reshape(PART, slots, WIDTH)
            if which == 0:
                block[parts, :CAP2] = d_key.astype(BF16)
                block[parts, CAP2 : 2 * CAP2] = d_value.astype(BF16)
            else:
                third = [d_key[:, :CAP3], d_value[:, :CAP3]]
        columns = columns_ref[i * PART * COLS : (i + 1) * PART * COLS]
        own = mm(columns, attended, NN).reshape(PART, COLS, WIDTH)
        block[parts, 2 * CAP2 :] = jnp.concatenate([*third, own], axis=1).astype(BF16)
        sends.append(pltpu.make_async_copy(block.at[parts], out_any.at[parts], sems.at[i]))
        sends[-1].start()
    for send in sends:
        send.wait()


def partial_kernel(kv_ref, dscore2_ref, dscore3_ref, out_ref):
    start = 0
    for (key, _), dscore_ref in zip(unpacked(kv_ref), (dscore2_ref, dscore3_ref)):
        count = dscore_ref.shape[1] // 2
        out_ref[start : start + count] = head_blocks(mm(dscore_ref[...], key, TN)) * SCALE
        start += count


def query_kernel(in_ref, dq_ref):
    _, y, _, c = place()
    near = y * NC + c
    second = pl.ds(pl.multiple_of(near * CAP2, CAP2), CAP2)
    third = pl.ds(pl.multiple_of(NEARS * CAP2 + near * PAD3, PAD3), PAD3)
    total = jnp.concatenate(
        [jnp.sum(in_ref[:, second, :], axis=0), jnp.sum(in_ref[:, third, :], axis=0)[:CAP3]], axis=0
    )
    dq_ref[...] = total.astype(BF16)


def last_kernel(in_ref, dk_ref, dv_ref, dw_ref):
    total = jnp.sum(in_ref[...].astype(F32), axis=0)
    third = 2 * CAP2
    dk_ref[...] = jnp.concatenate([total[:CAP2], total[third : third + CAP3]], axis=0).astype(BF16)
    dv_ref[...] = jnp.concatenate(
        [total[CAP2 : 2 * CAP2], total[third + CAP3 : third + 2 * CAP3]], axis=0
    ).astype(BF16)
    dw_ref[...] = total[third + PAD3 :]


def on_device(token_picks, live_counts, attn_query, attn_key, attn_value, out_grad, out_weight):
    del token_picks
    vmem = pl.BlockSpec(memory_space=pltpu.VMEM)
    anywhere = pl.BlockSpec(memory_space=pl.ANY)
    parameters = pltpu.CompilerParams(vmem_limit_bytes=32 * 2**20)

    def run(kernel, outs, args):
        return pl.pallas_call(
            kernel,
            out_shape=[jax.ShapeDtypeStruct(*o) for o in outs],
            in_specs=[vmem] * len(args),
            out_specs=[vmem] * len(outs),
            compiler_params=parameters,
        )(*args)

    live_counts = live_counts.T
    other = lax.ppermute(out_grad, "tp", [(0, 1), (1, 0), (2, 3), (3, 2)])
    kv, live, limits = pl.pallas_call(
        start_kernel,
        out_shape=[
            jax.ShapeDtypeStruct((NF, 2 * SLOTS, WIDTH), BF16),
            jax.ShapeDtypeStruct((ROWS, HS), F32),
            jax.ShapeDtypeStruct((2 * NF, HS), jnp.int32),
        ],
        in_specs=[anywhere] * 3,
        out_specs=[anywhere] * 3,
        scratch_shapes=[
            pltpu.SMEM(live_counts.shape, jnp.int32),
            pltpu.VMEM((SLOTS, WIDTH), BF16),
            pltpu.VMEM((SLOTS, WIDTH), BF16),
            pltpu.VMEM((BATCH, 2 * SLOTS, WIDTH), BF16),
            pltpu.VMEM((ROWS, HS), F32),
            pltpu.VMEM((2 * NF, HS), jnp.int32),
            pltpu.SemaphoreType.DMA((3,)),
            pltpu.SemaphoreType.DMA((NF // BATCH + 2,)),
        ],
    )(live_counts, attn_key, attn_value)
    kv = lax.all_to_all(kv, "seq", 0, 0, axis_index_groups=far_groups())
    (grad,) = pl.pallas_call(
        pair_kernel,
        out_shape=[jax.ShapeDtypeStruct((2, *out_grad.shape), BF16)],
        in_specs=[vmem] * 2,
        out_specs=[vmem],
        compiler_params=parameters,
        cost_estimate=pl.CostEstimate(flops=10**11, bytes_accessed=10**8, transcendentals=0),
    )(out_grad, other)
    grad = lax.all_gather(grad, "tp", axis=0, tiled=True, axis_index_groups=[[0, 3], [1, 2]])
    (qd,) = run(
        project_kernel, [((ROWS, 2 * WIDTH + MODEL), BF16)], (live, grad, out_weight, attn_query)
    )
    qd = lax.all_gather(qd, "seq", axis=0, tiled=False, axis_index_groups=near_groups())
    kinds = (CAP2, PAD3)
    tables = [(NF * slots, 2 * NEARS * slots) for slots in kinds]
    *ready, columns = run(
        prepare_kernel,
        [
            item
            for table in tables
            for item in (((table[1], WIDTH), BF16), ((table[1], WIDTH), BF16), (table, F32))
        ]
        + [((NF * COLS, QROWS), BF16)],
        (limits, qd),
    )
    stats, *kept = run(
        stats_kernel,
        [((QROWS + STATS, WIDTH), BF16)] + [(table, F32) for table in tables for _ in range(2)],
        (kv, *ready),
    )
    stats = lax.all_gather(stats, "seq", axis=0, tiled=False, axis_index_groups=near_groups())
    back, *dscores = pl.pallas_call(
        grads_kernel,
        out_shape=[jax.ShapeDtypeStruct((NF, BACK, WIDTH), BF16)]
        + [jax.ShapeDtypeStruct(table, BF16) for table in tables],
        in_specs=[vmem] * 10,
        out_specs=[anywhere, vmem, vmem],
        scratch_shapes=[pltpu.VMEM((NF, BACK, WIDTH), BF16), pltpu.SemaphoreType.DMA((NF // PART,))],
        compiler_params=parameters,
    )(stats, *ready[0:2], *ready[3:5], columns, *kept)
    back = lax.all_to_all(back, "seq", 0, 0, axis_index_groups=far_groups())
    (dq,) = run(partial_kernel, [((QROWS, WIDTH), F32)], (kv, *dscores))
    dq = lax.all_gather(dq, "seq", axis=0, tiled=False, axis_index_groups=near_groups())
    (query_grad,) = run(query_kernel, [((SLOTS, WIDTH), BF16)], (dq,))
    key_grad, value_grad, weight_grad = run(
        last_kernel,
        [((SLOTS, WIDTH), BF16), ((SLOTS, WIDTH), BF16), ((COLS, WIDTH), F32)],
        (back,),
    )
    return query_grad, key_grad, value_grad, weight_grad.T


def solution(mesh):
    rows = P("seq", "tp")
    return jax.shard_map(
        on_device,
        mesh=mesh,
        in_specs=(P(), P(), rows, rows, rows, rows, P("tp", None)),
        out_specs=(rows, rows, rows, P("tp", "seq")),
        check_vma=False,
    )
```

```python
import jax
import jax.numpy as jnp
from jax import lax
from jax.experimental import pallas as pl
from jax.experimental.pallas import tpu as pltpu
from jax.sharding import PartitionSpec as P

HS = 128
NZ, NY, NX, NC = 8, 2, 4, 2
NF, NEARS = NZ * NX, NY * NC
TP = 4
SLOTS = 20
CAP2 = 16
CAP3 = 4
PAD3 = 8
ROWS = CAP2 + PAD3
WIDTH = 2 * HS
MODEL = 2048
COLS = MODEL // 128
QROWS = NEARS * ROWS
BACK = 2 * CAP2 + PAD3 + COLS
PIECES = 3
STATS = 16
PART = 8
Z_ORDER = (7, 0, 1, 2, 3, 4, 5, 6)
BACK_ORDER = (0, 1, 2, 3, 28, 29, 30, 31, 24, 25, 26, 27, 20, 21, 22, 23, 16, 17, 18, 19, 12, 13, 14, 15, 8, 9, 10, 11, 4, 5, 6, 7)
BATCH = 8
SCALE = HS**-0.5
LOW = -1e30
F32 = jnp.float32
BF16 = jnp.bfloat16

NT = (((1,), (1,)), ((), ()))
NN = (((1,), (0,)), ((), ()))
TN = (((0,), (0,)), ((), ()))


def mm(left, right, dims):
    return lax.dot_general(left, right, dims, preferred_element_type=F32)


def split_rows(block):
    wide = block.astype(F32)
    count, _, width = wide.shape
    second = wide[:, :CAP2].reshape(count * CAP2, width).astype(BF16)
    third = wide[:, CAP2:].reshape(count * PAD3, width).astype(BF16)
    return second, third


def by_head(rows):
    column = lax.broadcasted_iota(jnp.int32, rows.shape, 1)
    zero = jnp.zeros_like(rows)
    return jnp.concatenate(
        [jnp.where(column < HS, rows, zero), jnp.where(column < HS, zero, rows)], axis=0
    )


def head_blocks(both):
    count = both.shape[0] // 2
    column = lax.broadcasted_iota(jnp.int32, (count, WIDTH), 1)
    return jnp.where(column < HS, both[:count], both[count:])


def shard_of(z, y, x, c):
    return ((z * NY + y) * NX + x) * NC + c


def place():
    index = lax.axis_index("seq")
    return index // (NY * NX * NC), index // (NX * NC) % NY, index // NC % NX, index % NC


def far_place(index):
    step = index // NX
    return sum((step == i) * z for i, z in enumerate(Z_ORDER)), index % NX


def far_groups(order):
    return [
        [shard_of(far_place(f)[0], y, far_place(f)[1], c) for f in order]
        for y in range(NY)
        for c in range(NC)
    ]


def near_groups():
    return [
        [shard_of(z, n // NC, x, n % NC) for n in range(NEARS)] for z in range(NZ) for x in range(NX)
    ]


def allowed(limit_ref, which, slots):
    z, y, x, c = place()
    shape = (NF * slots, 2 * NEARS * slots)
    key_row = lax.broadcasted_iota(jnp.int32, shape, 0)
    query_row = lax.broadcasted_iota(jnp.int32, shape, 1) % (NEARS * slots)
    key_far, key_slot = key_row // slots, key_row % slots
    key_z, key_x = far_place(key_far)
    key_shard = shard_of(key_z, y, key_x, c)
    near, query_slot = query_row // slots, query_row % slots
    query_shard = shard_of(z, near // NC, x, near % NC)
    limit = limit_ref[which * NF : (which + 1) * NF, : shape[1]]
    limit = jnp.broadcast_to(limit[:, None, :], (NF, slots, shape[1])).reshape(shape)
    in_order = key_shard * slots + key_slot <= query_shard * slots + query_slot
    return in_order & (key_slot < limit)


def padded(block):
    rest = jnp.zeros((ROWS - SLOTS, block.shape[1]), F32)
    return jnp.concatenate([block.astype(F32), rest], axis=0).astype(BF16)


def start_kernel(
    counts_any, key_any, value_any, kv_any, live_any, limit_any, counts, key, value, block, live, limits, sems, out_sems
):
    moves = [
        pltpu.make_async_copy(source, target, sems.at[i])
        for i, (source, target) in enumerate(((key_any, key), (value_any, value), (counts_any, counts)))
    ]
    for move in moves:
        move.start()
    moves[0].wait()
    moves[1].wait()
    keys, values = key[...].astype(F32), value[...].astype(F32)
    packed = jnp.concatenate(
        [keys[:CAP2], values[:CAP2], keys[CAP2:], values[CAP2:]], axis=0
    ).astype(BF16)
    for i in range(BATCH):
        block[i] = packed
    batches = NF // BATCH
    sends = [
        pltpu.make_async_copy(block, kv_any.at[i * BATCH : (i + 1) * BATCH], out_sems.at[i])
        for i in range(batches)
    ]
    for send in sends:
        send.start()
    moves[2].wait()
    z, y, x, c = place()
    shard = shard_of(z, y, x, c)
    slot = lax.broadcasted_iota(jnp.int32, live.shape, 0)
    limit = jnp.where(slot < CAP2, counts[0, shard], CAP2 + counts[1, shard])
    live[...] = jnp.where(slot < limit, 1.0, 0.0)
    for which in range(2):
        for f in range(NF):
            far_z, far_x = far_place(f)
            limit = counts[which, shard_of(far_z, y, far_x, c)]
            limits[which * NF + f : which * NF + f + 1, :] = jnp.full((1, HS), limit, jnp.int32)
    rest = [
        pltpu.make_async_copy(live, live_any, out_sems.at[batches]),
        pltpu.make_async_copy(limits, limit_any, out_sems.at[batches + 1]),
    ]
    for send in rest:
        send.start()
    for send in sends + rest:
        send.wait()


def pair_kernel(own_ref, other_ref, out_ref):
    out_ref[0] = own_ref[...]
    out_ref[1] = other_ref[...]


def project_kernel(live_ref, grad_ref, weight_ref, query_ref, out_ref):
    me = lax.axis_index("tp")
    outer = (me == 0) | (me == 3)
    first, second = jnp.where(outer, 0, 1), jnp.where(outer, 3, 2)
    live = live_ref[:, :1]
    total = jnp.zeros((ROWS, WIDTH), F32)
    for k, t in enumerate((first, 1 - first, second, 5 - second)):
        column = pl.multiple_of(t * 512, 512)
        wide = jnp.concatenate(
            [grad_ref[k].astype(F32), jnp.zeros((ROWS - SLOTS, 512), F32)], axis=0
        )
        piece = (wide * live).astype(BF16)
        total += mm(piece, weight_ref[:, pl.ds(column, 512)], NT)
        out_ref[:, pl.ds(2 * WIDTH + column, 512)] = piece
    out_ref[:, :WIDTH] = padded(query_ref[...])
    out_ref[:, WIDTH : 2 * WIDTH] = total.astype(BF16)


def prepare_kernel(limit_ref, qd_ref, *refs):
    _, y, _, c = place()
    qd_parts = split_rows(qd_ref[:, :, : 2 * WIDTH])
    for which, slots in ((0, CAP2), (1, PAD3)):
        query_ref, d_attn_ref, bias_ref = refs[3 * which : 3 * which + 3]
        query_ref[...] = by_head(qd_parts[which][:, :WIDTH])
        d_attn_ref[...] = by_head(qd_parts[which][:, WIDTH:])
        bias_ref[...] = jnp.where(allowed(limit_ref, which, slots), 0.0, LOW)
    columns_ref = refs[6]
    for step in range(NZ):
        z, _ = far_place(step * NX)
        column = pl.multiple_of(2 * WIDTH + (z * NY + y) * HS, HS)
        wide = qd_ref[:, :, pl.ds(column, HS)].astype(F32)
        rows = jnp.concatenate(
            [wide[:, :CAP2].reshape(NEARS * CAP2, HS), wide[:, CAP2:].reshape(NEARS * PAD3, HS)], axis=0
        )
        down = rows.T.reshape(NX, NC, COLS, QROWS)
        own = jnp.where(c == 0, down[:, 0], down[:, 1]).reshape(NX * COLS, QROWS)
        columns_ref[step * NX * COLS : (step + 1) * NX * COLS] = own.astype(BF16)


def unpacked(kv_ref):
    third = kv_ref[:, 2 * CAP2 :].astype(F32)
    shifted = jnp.concatenate([third[:, CAP3:], third[:, :CAP3]], axis=1)
    second = (kv_ref[:, :CAP2].reshape(NF * CAP2, WIDTH), kv_ref[:, CAP2 : 2 * CAP2].reshape(NF * CAP2, WIDTH))
    return (second, tuple(part.reshape(NF * PAD3, WIDTH).astype(BF16) for part in (third, shifted)))


def stats_kernel(kv_ref, *refs):
    ready, out_ref, kept = refs[:6], refs[6], refs[7:]
    kv = unpacked(kv_ref)
    start = 0
    stats = []
    for which, slots in ((0, CAP2), (1, PAD3)):
        key, value = kv[which]
        query, d_attn, bias = (ref[...] for ref in ready[3 * which : 3 * which + 3])
        scores = mm(key, query, NT) * SCALE + bias
        dprob = mm(value, d_attn, NT)
        kept[2 * which][...] = scores
        kept[2 * which + 1][...] = dprob
        top = jnp.max(scores, axis=0, keepdims=True)
        weights = jnp.exp(scores - top)
        total = jnp.sum(weights, axis=0, keepdims=True)
        weights = weights * (1.0 / total)
        logs = jnp.where(top < 0.5 * LOW, LOW, top + jnp.log(total))
        delta = jnp.sum(weights * dprob, axis=0, keepdims=True)
        attended = head_blocks(mm(weights.astype(BF16), value, TN))
        out_ref[start : start + NEARS * slots] = attended.astype(BF16)
        start += NEARS * slots
        for row in (logs, delta):
            row = jnp.concatenate([row, jnp.zeros((1, WIDTH - row.shape[1]), F32)], axis=1)
            for _ in range(PIECES):
                piece = row.astype(BF16).astype(F32)
                stats.append(piece)
                row = row - piece
    rest = jnp.zeros((STATS - len(stats), WIDTH), F32)
    out_ref[start:] = jnp.concatenate(stats + [rest], axis=0).astype(BF16)


def grads_kernel(in_ref, *refs):
    ready, columns_ref, kept, out_any, dscore_refs = refs[:4], refs[4], refs[5:9], refs[9], refs[10:12]
    block, sems = refs[12:]
    lines = in_ref[:, QROWS:].astype(F32)
    attended, totals = [], []
    start = 0
    for which, slots in ((0, CAP2), (1, PAD3)):
        count = NEARS * slots
        logs, deltas = (
            jnp.sum(lines[:, first : first + PIECES, : 2 * count], axis=1)
            for first in (2 * which * PIECES, (2 * which + 1) * PIECES)
        )
        top = jnp.max(logs, axis=0, keepdims=True)
        log_total = top + jnp.log(jnp.sum(jnp.exp(logs - top), axis=0, keepdims=True))
        share = jnp.exp(logs - log_total)
        totals.append((log_total, jnp.sum(share * deltas, axis=0, keepdims=True)))
        share_down = jnp.concatenate([share, jnp.zeros((8 - NEARS, 2 * count), F32)], axis=0).T
        column = lax.broadcasted_iota(jnp.int32, (count, WIDTH), 1)
        total = jnp.zeros((count, WIDTH), F32)
        for n in range(NEARS):
            own = jnp.where(column < HS, share_down[:count, n : n + 1], share_down[count:, n : n + 1])
            total += own * in_ref[n, start : start + count].astype(F32)
        attended.append(total)
        start += count
    attended = jnp.concatenate(attended, axis=0).astype(BF16)

    for which, slots in ((0, CAP2), (1, PAD3)):
        query, d_attn = (ref[...] for ref in ready[2 * which : 2 * which + 2])
        log_total, delta = totals[which]
        prob = jnp.exp(kept[2 * which][...] - log_total)
        dscore = (prob * (kept[2 * which + 1][...] - delta)).astype(BF16)
        dscore_refs[which][...] = dscore
        d_key = (mm(dscore, query, NN) * SCALE).reshape(NF, slots, WIDTH)
        d_value = mm(prob.astype(BF16), d_attn, NN).reshape(NF, slots, WIDTH)
        if which == 0:
            for message, f in enumerate(BACK_ORDER):
                block[message, :CAP2] = d_key[f].astype(BF16)
                block[message, CAP2 : 2 * CAP2] = d_value[f].astype(BF16)
        else:
            third = jnp.concatenate([d_key[:, :CAP3], d_value[:, :CAP3]], axis=1)
    own = mm(columns_ref[...], attended, NN).reshape(NF, COLS, WIDTH)
    third = jnp.concatenate([third, own], axis=1).astype(BF16)
    sends = []
    for i in range(NF // PART):
        for message in range(i * PART, (i + 1) * PART):
            block[message, 2 * CAP2 :] = third[BACK_ORDER[message]]
        parts = slice(i * PART, (i + 1) * PART)
        sends.append(pltpu.make_async_copy(block.at[parts], out_any.at[parts], sems.at[i]))
        sends[-1].start()
    for send in sends:
        send.wait()


def partial_kernel(kv_ref, dscore2_ref, dscore3_ref, out_ref):
    start = 0
    for (key, _), dscore_ref in zip(unpacked(kv_ref), (dscore2_ref, dscore3_ref)):
        count = dscore_ref.shape[1] // 2
        out_ref[start : start + count] = head_blocks(mm(dscore_ref[...], key, TN)) * SCALE
        start += count


def query_kernel(in_ref, dq_ref):
    _, y, _, c = place()
    near = y * NC + c
    second = pl.ds(pl.multiple_of(near * CAP2, CAP2), CAP2)
    third = pl.ds(pl.multiple_of(NEARS * CAP2 + near * PAD3, PAD3), PAD3)
    total = jnp.concatenate(
        [jnp.sum(in_ref[:, second, :], axis=0), jnp.sum(in_ref[:, third, :], axis=0)[:CAP3]], axis=0
    )
    dq_ref[...] = total.astype(BF16)


def last_kernel(in_ref, dk_ref, dv_ref, dw_ref):
    total = jnp.sum(in_ref[...].astype(F32), axis=0)
    third = 2 * CAP2
    dk_ref[...] = jnp.concatenate([total[:CAP2], total[third : third + CAP3]], axis=0).astype(BF16)
    dv_ref[...] = jnp.concatenate(
        [total[CAP2 : 2 * CAP2], total[third + CAP3 : third + 2 * CAP3]], axis=0
    ).astype(BF16)
    dw_ref[...] = total[third + PAD3 :]


def on_device(token_picks, live_counts, attn_query, attn_key, attn_value, out_grad, out_weight):
    del token_picks
    vmem = pl.BlockSpec(memory_space=pltpu.VMEM)
    anywhere = pl.BlockSpec(memory_space=pl.ANY)
    parameters = pltpu.CompilerParams(vmem_limit_bytes=32 * 2**20)

    def run(kernel, outs, args):
        return pl.pallas_call(
            kernel,
            out_shape=[jax.ShapeDtypeStruct(*o) for o in outs],
            in_specs=[vmem] * len(args),
            out_specs=[vmem] * len(outs),
            compiler_params=parameters,
        )(*args)

    live_counts = live_counts.T
    other = lax.ppermute(out_grad, "tp", [(0, 1), (1, 0), (2, 3), (3, 2)])
    kv, live, limits = pl.pallas_call(
        start_kernel,
        out_shape=[
            jax.ShapeDtypeStruct((NF, 2 * SLOTS, WIDTH), BF16),
            jax.ShapeDtypeStruct((ROWS, HS), F32),
            jax.ShapeDtypeStruct((2 * NF, HS), jnp.int32),
        ],
        in_specs=[anywhere] * 3,
        out_specs=[anywhere] * 3,
        scratch_shapes=[
            pltpu.SMEM(live_counts.shape, jnp.int32),
            pltpu.VMEM((SLOTS, WIDTH), BF16),
            pltpu.VMEM((SLOTS, WIDTH), BF16),
            pltpu.VMEM((BATCH, 2 * SLOTS, WIDTH), BF16),
            pltpu.VMEM((ROWS, HS), F32),
            pltpu.VMEM((2 * NF, HS), jnp.int32),
            pltpu.SemaphoreType.DMA((3,)),
            pltpu.SemaphoreType.DMA((NF // BATCH + 2,)),
        ],
    )(live_counts, attn_key, attn_value)
    kv = lax.all_to_all(kv, "seq", 0, 0, axis_index_groups=far_groups(range(NF)))
    (grad,) = pl.pallas_call(
        pair_kernel,
        out_shape=[jax.ShapeDtypeStruct((2, *out_grad.shape), BF16)],
        in_specs=[vmem] * 2,
        out_specs=[vmem],
        compiler_params=parameters,
        cost_estimate=pl.CostEstimate(flops=10**11, bytes_accessed=10**8, transcendentals=0),
    )(out_grad, other)
    grad = lax.all_gather(grad, "tp", axis=0, tiled=True, axis_index_groups=[[0, 3], [1, 2]])
    (qd,) = run(
        project_kernel, [((ROWS, 2 * WIDTH + MODEL), BF16)], (live, grad, out_weight, attn_query)
    )
    qd = lax.all_gather(qd, "seq", axis=0, tiled=False, axis_index_groups=near_groups())
    kinds = (CAP2, PAD3)
    tables = [(NF * slots, 2 * NEARS * slots) for slots in kinds]
    *ready, columns = run(
        prepare_kernel,
        [
            item
            for table in tables
            for item in (((table[1], WIDTH), BF16), ((table[1], WIDTH), BF16), (table, F32))
        ]
        + [((NF * COLS, QROWS), BF16)],
        (limits, qd),
    )
    stats, *kept = run(
        stats_kernel,
        [((QROWS + STATS, WIDTH), BF16)] + [(table, F32) for table in tables for _ in range(2)],
        (kv, *ready),
    )
    stats = lax.all_gather(stats, "seq", axis=0, tiled=False, axis_index_groups=near_groups())
    back, *dscores = pl.pallas_call(
        grads_kernel,
        out_shape=[jax.ShapeDtypeStruct((NF, BACK, WIDTH), BF16)]
        + [jax.ShapeDtypeStruct(table, BF16) for table in tables],
        in_specs=[vmem] * 10,
        out_specs=[anywhere, vmem, vmem],
        scratch_shapes=[pltpu.VMEM((NF, BACK, WIDTH), BF16), pltpu.SemaphoreType.DMA((NF // PART,))],
        compiler_params=parameters,
    )(stats, *ready[0:2], *ready[3:5], columns, *kept)
    back = lax.all_to_all(back, "seq", 0, 0, axis_index_groups=far_groups(BACK_ORDER))
    (dq,) = run(partial_kernel, [((QROWS, WIDTH), F32)], (kv, *dscores))
    dq = lax.all_gather(dq, "seq", axis=0, tiled=False, axis_index_groups=near_groups())
    (query_grad,) = run(query_kernel, [((SLOTS, WIDTH), BF16)], (dq,))
    key_grad, value_grad, weight_grad = run(
        last_kernel,
        [((SLOTS, WIDTH), BF16), ((SLOTS, WIDTH), BF16), ((COLS, WIDTH), F32)],
        (back,),
    )
    return query_grad, key_grad, value_grad, weight_grad.T


def solution(mesh):
    rows = P("seq", "tp")
    return jax.shard_map(
        on_device,
        mesh=mesh,
        in_specs=(P(), P(), rows, rows, rows, rows, P("tp", None)),
        out_specs=(rows, rows, rows, P("tp", "seq")),
        check_vma=False,
    )
```

```python
import jax
import jax.numpy as jnp
from jax import lax
from jax.experimental import pallas as pl
from jax.experimental.pallas import tpu as pltpu
from jax.sharding import PartitionSpec as P

HS = 128
NZ, NY, NX, NC = 8, 2, 4, 2
NF, NEARS = NZ * NX, NY * NC
TP = 4
SLOTS = 20
CAP2 = 16
CAP3 = 4
PAD3 = 8
ROWS = CAP2 + PAD3
WIDTH = 2 * HS
MODEL = 2048
COLS = MODEL // 128
QROWS = NEARS * ROWS
BACK = 2 * CAP2 + PAD3 + COLS
PIECES = 3
STATS = 16
PART = 4
BATCH = 8
SCALE = HS**-0.5
LOW = -1e30
F32 = jnp.float32
BF16 = jnp.bfloat16

NT = (((1,), (1,)), ((), ()))
NN = (((1,), (0,)), ((), ()))
TN = (((0,), (0,)), ((), ()))


def mm(left, right, dims):
    return lax.dot_general(left, right, dims, preferred_element_type=F32)


def split_rows(block):
    wide = block.astype(F32)
    count, _, width = wide.shape
    second = wide[:, :CAP2].reshape(count * CAP2, width).astype(BF16)
    third = wide[:, CAP2:].reshape(count * PAD3, width).astype(BF16)
    return second, third


def by_head(rows):
    column = lax.broadcasted_iota(jnp.int32, rows.shape, 1)
    zero = jnp.zeros_like(rows)
    return jnp.concatenate(
        [jnp.where(column < HS, rows, zero), jnp.where(column < HS, zero, rows)], axis=0
    )


def head_blocks(both):
    count = both.shape[0] // 2
    column = lax.broadcasted_iota(jnp.int32, (count, WIDTH), 1)
    return jnp.where(column < HS, both[:count], both[count:])


def shard_of(z, y, x, c):
    return ((z * NY + y) * NX + x) * NC + c


def place():
    index = lax.axis_index("seq")
    return index // (NY * NX * NC), index // (NX * NC) % NY, index // NC % NX, index % NC


def far_place(index):
    step = index // NX
    return step - 1 + NZ * (step == 0), index % NX


def message_of(index):
    z, x = far_place(index)
    return (NZ - 1 - z) * NX + x


def far_groups(order):
    return [
        [shard_of(far_place(f)[0], y, far_place(f)[1], c) for f in order]
        for y in range(NY)
        for c in range(NC)
    ]


def near_groups():
    return [
        [shard_of(z, n // NC, x, n % NC) for n in range(NEARS)] for z in range(NZ) for x in range(NX)
    ]


def allowed(limit_ref, which, slots):
    z, y, x, c = place()
    shape = (NF * slots, 2 * NEARS * slots)
    key_row = lax.broadcasted_iota(jnp.int32, shape, 0)
    query_row = lax.broadcasted_iota(jnp.int32, shape, 1) % (NEARS * slots)
    key_far, key_slot = key_row // slots, key_row % slots
    key_z, key_x = far_place(key_far)
    key_shard = shard_of(key_z, y, key_x, c)
    near, query_slot = query_row // slots, query_row % slots
    query_shard = shard_of(z, near // NC, x, near % NC)
    limit = limit_ref[which * NF : (which + 1) * NF, : shape[1]]
    limit = jnp.broadcast_to(limit[:, None, :], (NF, slots, shape[1])).reshape(shape)
    in_order = key_shard * slots + key_slot <= query_shard * slots + query_slot
    return in_order & (key_slot < limit)


def padded(block):
    rest = jnp.zeros((ROWS - SLOTS, block.shape[1]), F32)
    return jnp.concatenate([block.astype(F32), rest], axis=0).astype(BF16)


def start_kernel(
    counts_any, key_any, value_any, kv_any, live_any, limit_any, counts, key, value, block, live, limits, sems, out_sems
):
    moves = [
        pltpu.make_async_copy(source, target, sems.at[i])
        for i, (source, target) in enumerate(((key_any, key), (value_any, value), (counts_any, counts)))
    ]
    for move in moves:
        move.start()
    moves[0].wait()
    moves[1].wait()
    keys, values = key[...].astype(F32), value[...].astype(F32)
    packed = jnp.concatenate(
        [keys[:CAP2], values[:CAP2], keys[CAP2:], values[CAP2:]], axis=0
    ).astype(BF16)
    for i in range(BATCH):
        block[i] = packed
    batches = NF // BATCH
    sends = [
        pltpu.make_async_copy(block, kv_any.at[i * BATCH : (i + 1) * BATCH], out_sems.at[i])
        for i in range(batches)
    ]
    for send in sends:
        send.start()
    moves[2].wait()
    z, y, x, c = place()
    shard = shard_of(z, y, x, c)
    slot = lax.broadcasted_iota(jnp.int32, live.shape, 0)
    limit = jnp.where(slot < CAP2, counts[0, shard], CAP2 + counts[1, shard])
    live[...] = jnp.where(slot < limit, 1.0, 0.0)
    for which in range(2):
        for f in range(NF):
            far_z, far_x = far_place(f)
            limit = counts[which, shard_of(far_z, y, far_x, c)]
            limits[which * NF + f : which * NF + f + 1, :] = jnp.full((1, HS), limit, jnp.int32)
    rest = [
        pltpu.make_async_copy(live, live_any, out_sems.at[batches]),
        pltpu.make_async_copy(limits, limit_any, out_sems.at[batches + 1]),
    ]
    for send in rest:
        send.start()
    for send in sends + rest:
        send.wait()


def pair_kernel(own_ref, other_ref, out_ref):
    out_ref[0] = own_ref[...]
    out_ref[1] = other_ref[...]


def project_kernel(live_ref, grad_ref, weight_ref, query_ref, out_ref):
    me = lax.axis_index("tp")
    outer = (me == 0) | (me == 3)
    first, second = jnp.where(outer, 0, 1), jnp.where(outer, 3, 2)
    live = live_ref[:, :1]
    total = jnp.zeros((ROWS, WIDTH), F32)
    for k, t in enumerate((first, 1 - first, second, 5 - second)):
        column = pl.multiple_of(t * 512, 512)
        wide = jnp.concatenate(
            [grad_ref[k].astype(F32), jnp.zeros((ROWS - SLOTS, 512), F32)], axis=0
        )
        piece = (wide * live).astype(BF16)
        total += mm(piece, weight_ref[:, pl.ds(column, 512)], NT)
        out_ref[:, pl.ds(2 * WIDTH + column, 512)] = piece
    out_ref[:, :WIDTH] = padded(query_ref[...])
    out_ref[:, WIDTH : 2 * WIDTH] = total.astype(BF16)


def prepare_kernel(limit_ref, qd_ref, *refs):
    _, y, _, c = place()
    qd_parts = split_rows(qd_ref[:, :, : 2 * WIDTH])
    for which, slots in ((0, CAP2), (1, PAD3)):
        query_ref, d_attn_ref, bias_ref = refs[3 * which : 3 * which + 3]
        query_ref[...] = by_head(qd_parts[which][:, :WIDTH])
        d_attn_ref[...] = by_head(qd_parts[which][:, WIDTH:])
        bias_ref[...] = jnp.where(allowed(limit_ref, which, slots), 0.0, LOW)
    columns_ref = refs[6]
    for step in range(NZ):
        z, _ = far_place(step * NX)
        column = pl.multiple_of(2 * WIDTH + (z * NY + y) * HS, HS)
        wide = qd_ref[:, :, pl.ds(column, HS)].astype(F32)
        rows = jnp.concatenate(
            [wide[:, :CAP2].reshape(NEARS * CAP2, HS), wide[:, CAP2:].reshape(NEARS * PAD3, HS)], axis=0
        )
        down = rows.T.reshape(NX, NC, COLS, QROWS)
        own = jnp.where(c == 0, down[:, 0], down[:, 1]).reshape(NX * COLS, QROWS)
        columns_ref[step * NX * COLS : (step + 1) * NX * COLS] = own.astype(BF16)


def unpacked(kv_ref):
    third = kv_ref[:, 2 * CAP2 :].astype(F32)
    shifted = jnp.concatenate([third[:, CAP3:], third[:, :CAP3]], axis=1)
    second = (kv_ref[:, :CAP2].reshape(NF * CAP2, WIDTH), kv_ref[:, CAP2 : 2 * CAP2].reshape(NF * CAP2, WIDTH))
    return (second, tuple(part.reshape(NF * PAD3, WIDTH).astype(BF16) for part in (third, shifted)))


def stats_kernel(kv_ref, *refs):
    ready, out_ref, kept = refs[:6], refs[6], refs[7:]
    kv = unpacked(kv_ref)
    start = 0
    stats = []
    for which, slots in ((0, CAP2), (1, PAD3)):
        key, value = kv[which]
        query, d_attn, bias = (ref[...] for ref in ready[3 * which : 3 * which + 3])
        scores = mm(key, query, NT) * SCALE + bias
        dprob = mm(value, d_attn, NT)
        kept[2 * which][...] = scores
        kept[2 * which + 1][...] = dprob
        top = jnp.max(scores, axis=0, keepdims=True)
        weights = jnp.exp(scores - top)
        total = jnp.sum(weights, axis=0, keepdims=True)
        weights = weights * (1.0 / total)
        logs = jnp.where(top < 0.5 * LOW, LOW, top + jnp.log(total))
        delta = jnp.sum(weights * dprob, axis=0, keepdims=True)
        attended = head_blocks(mm(weights.astype(BF16), value, TN))
        out_ref[start : start + NEARS * slots] = attended.astype(BF16)
        start += NEARS * slots
        for row in (logs, delta):
            row = jnp.concatenate([row, jnp.zeros((1, WIDTH - row.shape[1]), F32)], axis=1)
            for _ in range(PIECES):
                piece = row.astype(BF16).astype(F32)
                stats.append(piece)
                row = row - piece
    rest = jnp.zeros((STATS - len(stats), WIDTH), F32)
    out_ref[start:] = jnp.concatenate(stats + [rest], axis=0).astype(BF16)


def grads_kernel(in_ref, *refs):
    ready, columns_ref, kept, out_any, dscore_refs = refs[:4], refs[4], refs[5:9], refs[9], refs[10:12]
    block, sems = refs[12:]
    lines = in_ref[:, QROWS:].astype(F32)
    attended, totals = [], []
    start = 0
    for which, slots in ((0, CAP2), (1, PAD3)):
        count = NEARS * slots
        logs, deltas = (
            jnp.sum(lines[:, first : first + PIECES, : 2 * count], axis=1)
            for first in (2 * which * PIECES, (2 * which + 1) * PIECES)
        )
        top = jnp.max(logs, axis=0, keepdims=True)
        log_total = top + jnp.log(jnp.sum(jnp.exp(logs - top), axis=0, keepdims=True))
        share = jnp.exp(logs - log_total)
        totals.append((log_total, jnp.sum(share * deltas, axis=0, keepdims=True)))
        share_down = jnp.concatenate([share, jnp.zeros((8 - NEARS, 2 * count), F32)], axis=0).T
        column = lax.broadcasted_iota(jnp.int32, (count, WIDTH), 1)
        total = jnp.zeros((count, WIDTH), F32)
        for n in range(NEARS):
            own = jnp.where(column < HS, share_down[:count, n : n + 1], share_down[count:, n : n + 1])
            total += own * in_ref[n, start : start + count].astype(F32)
        attended.append(total)
        start += count
    attended = jnp.concatenate(attended, axis=0).astype(BF16)

    sends = []
    for i in range(NF // PART):
        first = message_of(i * PART)
        parts = slice(first, first + PART)
        third = []
        for which, slots in ((0, CAP2), (1, PAD3)):
            query, d_attn = (ref[...] for ref in ready[2 * which : 2 * which + 2])
            log_total, delta = totals[which]
            keys = slice(i * PART * slots, (i + 1) * PART * slots)
            prob = jnp.exp(kept[2 * which][keys] - log_total)
            dscore = (prob * (kept[2 * which + 1][keys] - delta)).astype(BF16)
            dscore_refs[which][keys] = dscore
            d_key = (mm(dscore, query, NN) * SCALE).reshape(PART, slots, WIDTH)
            d_value = mm(prob.astype(BF16), d_attn, NN).reshape(PART, slots, WIDTH)
            if which == 0:
                block[parts, :CAP2] = d_key.astype(BF16)
                block[parts, CAP2 : 2 * CAP2] = d_value.astype(BF16)
            else:
                third = [d_key[:, :CAP3], d_value[:, :CAP3]]
        columns = columns_ref[i * PART * COLS : (i + 1) * PART * COLS]
        own = mm(columns, attended, NN).reshape(PART, COLS, WIDTH)
        block[parts, 2 * CAP2 :] = jnp.concatenate([*third, own], axis=1).astype(BF16)
        sends.append(pltpu.make_async_copy(block.at[parts], out_any.at[parts], sems.at[i]))
        sends[-1].start()
    for send in sends:
        send.wait()


def partial_kernel(kv_ref, dscore2_ref, dscore3_ref, out_ref):
    start = 0
    for (key, _), dscore_ref in zip(unpacked(kv_ref), (dscore2_ref, dscore3_ref)):
        count = dscore_ref.shape[1] // 2
        out_ref[start : start + count] = head_blocks(mm(dscore_ref[...], key, TN)) * SCALE
        start += count


def query_kernel(in_ref, dq_ref):
    _, y, _, c = place()
    near = y * NC + c
    second = pl.ds(pl.multiple_of(near * CAP2, CAP2), CAP2)
    third = pl.ds(pl.multiple_of(NEARS * CAP2 + near * PAD3, PAD3), PAD3)
    total = jnp.concatenate(
        [jnp.sum(in_ref[:, second, :], axis=0), jnp.sum(in_ref[:, third, :], axis=0)[:CAP3]], axis=0
    )
    dq_ref[...] = total.astype(BF16)


def last_kernel(in_ref, dk_ref, dv_ref, dw_ref):
    total = jnp.sum(in_ref[...].astype(F32), axis=0)
    third = 2 * CAP2
    dk_ref[...] = jnp.concatenate([total[:CAP2], total[third : third + CAP3]], axis=0).astype(BF16)
    dv_ref[...] = jnp.concatenate(
        [total[CAP2 : 2 * CAP2], total[third + CAP3 : third + 2 * CAP3]], axis=0
    ).astype(BF16)
    dw_ref[...] = total[third + PAD3 :]


def on_device(token_picks, live_counts, attn_query, attn_key, attn_value, out_grad, out_weight):
    del token_picks
    vmem = pl.BlockSpec(memory_space=pltpu.VMEM)
    anywhere = pl.BlockSpec(memory_space=pl.ANY)
    parameters = pltpu.CompilerParams(vmem_limit_bytes=32 * 2**20)

    def run(kernel, outs, args):
        return pl.pallas_call(
            kernel,
            out_shape=[jax.ShapeDtypeStruct(*o) for o in outs],
            in_specs=[vmem] * len(args),
            out_specs=[vmem] * len(outs),
            compiler_params=parameters,
        )(*args)

    live_counts = live_counts.T
    other = lax.ppermute(out_grad, "tp", [(0, 1), (1, 0), (2, 3), (3, 2)])
    kv, live, limits = pl.pallas_call(
        start_kernel,
        out_shape=[
            jax.ShapeDtypeStruct((NF, 2 * SLOTS, WIDTH), BF16),
            jax.ShapeDtypeStruct((ROWS, HS), F32),
            jax.ShapeDtypeStruct((2 * NF, HS), jnp.int32),
        ],
        in_specs=[anywhere] * 3,
        out_specs=[anywhere] * 3,
        scratch_shapes=[
            pltpu.SMEM(live_counts.shape, jnp.int32),
            pltpu.VMEM((SLOTS, WIDTH), BF16),
            pltpu.VMEM((SLOTS, WIDTH), BF16),
            pltpu.VMEM((BATCH, 2 * SLOTS, WIDTH), BF16),
            pltpu.VMEM((ROWS, HS), F32),
            pltpu.VMEM((2 * NF, HS), jnp.int32),
            pltpu.SemaphoreType.DMA((3,)),
            pltpu.SemaphoreType.DMA((NF // BATCH + 2,)),
        ],
    )(live_counts, attn_key, attn_value)
    kv = lax.all_to_all(kv, "seq", 0, 0, axis_index_groups=far_groups(range(NF)))
    (grad,) = pl.pallas_call(
        pair_kernel,
        out_shape=[jax.ShapeDtypeStruct((2, *out_grad.shape), BF16)],
        in_specs=[vmem] * 2,
        out_specs=[vmem],
        compiler_params=parameters,
        cost_estimate=pl.CostEstimate(flops=10**11, bytes_accessed=10**8, transcendentals=0),
    )(out_grad, other)
    grad = lax.all_gather(grad, "tp", axis=0, tiled=True, axis_index_groups=[[0, 3], [1, 2]])
    (qd,) = run(
        project_kernel, [((ROWS, 2 * WIDTH + MODEL), BF16)], (live, grad, out_weight, attn_query)
    )
    qd = lax.all_gather(qd, "seq", axis=0, tiled=False, axis_index_groups=near_groups())
    kinds = (CAP2, PAD3)
    tables = [(NF * slots, 2 * NEARS * slots) for slots in kinds]
    *ready, columns = run(
        prepare_kernel,
        [
            item
            for table in tables
            for item in (((table[1], WIDTH), BF16), ((table[1], WIDTH), BF16), (table, F32))
        ]
        + [((NF * COLS, QROWS), BF16)],
        (limits, qd),
    )
    stats, *kept = run(
        stats_kernel,
        [((QROWS + STATS, WIDTH), BF16)] + [(table, F32) for table in tables for _ in range(2)],
        (kv, *ready),
    )
    stats = lax.all_gather(stats, "seq", axis=0, tiled=False, axis_index_groups=near_groups())
    back, *dscores = pl.pallas_call(
        grads_kernel,
        out_shape=[jax.ShapeDtypeStruct((NF, BACK, WIDTH), BF16)]
        + [jax.ShapeDtypeStruct(table, BF16) for table in tables],
        in_specs=[vmem] * 10,
        out_specs=[anywhere, vmem, vmem],
        scratch_shapes=[pltpu.VMEM((NF, BACK, WIDTH), BF16), pltpu.SemaphoreType.DMA((NF // PART,))],
        compiler_params=parameters,
    )(stats, *ready[0:2], *ready[3:5], columns, *kept)
    back = lax.all_to_all(
        back, "seq", 0, 0, axis_index_groups=far_groups(sorted(range(NF), key=message_of))
    )
    (dq,) = run(partial_kernel, [((QROWS, WIDTH), F32)], (kv, *dscores))
    dq = lax.all_gather(dq, "seq", axis=0, tiled=False, axis_index_groups=near_groups())
    (query_grad,) = run(query_kernel, [((SLOTS, WIDTH), BF16)], (dq,))
    key_grad, value_grad, weight_grad = run(
        last_kernel,
        [((SLOTS, WIDTH), BF16), ((SLOTS, WIDTH), BF16), ((COLS, WIDTH), F32)],
        (back,),
    )
    return query_grad, key_grad, value_grad, weight_grad.T


def solution(mesh):
    rows = P("seq", "tp")
    return jax.shard_map(
        on_device,
        mesh=mesh,
        in_specs=(P(), P(), rows, rows, rows, rows, P("tp", None)),
        out_specs=(rows, rows, rows, P("tp", "seq")),
        check_vma=False,
    )
```
